256 devices in a mesh: cuts: 16 (over x, y_hi, core), fsdp: 16 (over z, y_lo).
Axes of the slice: x: 4, y: 4 (y_hi: 2, y_lo: 2; y = y_hi * 2 + y_lo), z: 8, core: 2. Of those that a mesh axis runs over, the one named last changes fastest.
Arguments:
- layer_input: bfloat16 [131072, 8192], P(('cuts', 'fsdp')), may hold values from -6 to 6
- value_cotangent: bfloat16 [131072, 512], P(('cuts', 'fsdp')), may hold values from -0.015625 to 0.015625
- master_weight: float32 [8192, 512], P('fsdp'), may hold values from -0.0068359375 to 0.0068359375
- first_moment: float32 [8192, 512], P('fsdp'), may hold values from -0.3125 to 0.3125
- second_moment: float32 [8192, 512], P('fsdp'), may hold values from 0.05 to 1
- next_input: bfloat16 [32768, 8192], P(('cuts', 'fsdp')), may hold values from -6 to 6
Outputs:
- new_master: float32 [8192, 512], P('fsdp')
- new_first: float32 [8192, 512], P('fsdp')
- new_second: float32 [8192, 512], P('fsdp')
- next_values: bfloat16 [32768, 512], P(('cuts', 'fsdp'))
The draws below stay inside these ranges and needn't reach their ends.
All inputs are finite; a program needn't handle non-finite values.
Results may differ from the reference program's by a relative error of at most 0.005.
Values may be sent and summed in bfloat16 or wider, within the bound.
A program may use at most 128 MiB of HBM per device.

```python
import math
import jax
import jax.numpy as jnp
from jax import lax

D = 8192
KV = 512
STEP = 200
TOKENS = 131072
NEXT_TOKENS = 32768


def block_levels(stream_key, extent, split, smallest, high):
    factor_of, own = 1.0, jax.random.fold_in(stream_key, 6)
    for position, shards_of in split:
        steps = jnp.exp(jax.random.uniform(jax.random.fold_in(own, position), (shards_of,), jnp.float32, smallest / len(split), high / len(split)))
        factor_of = factor_of * jnp.repeat(steps, extent[position] // shards_of).reshape([-1 if axis == position else 1 for axis in range(len(extent))])
    return factor_of


def normal_values(rng, extent, deviation, reach, shards=(), held_as=jnp.bfloat16):
    array = jax.random.normal(rng, extent, jnp.float32) * deviation
    if len(shards) > 0:
        array = block_levels(rng, extent, shards, -0.22, 0.18) * array
    return jnp.clip(array, min=-reach, max=reach).astype(held_as)


def setup_inputs(seed: int = 0) -> dict:
    splits = jax.random.split(jax.random.key(seed), 7)
    layer_input = normal_values(splits[0], (TOKENS, D), 1.0, 6.0, ((0, 256),))
    value_cotangent = normal_values(splits[1], (TOKENS, KV), TOKENS ** -0.5, 0.015625, ((0, 256),))
    master_weight = normal_values(splits[2], (D, KV), (100 * D) ** -0.5, 0.0068359375, ((0, 16),), jnp.float32)
    first_moment = normal_values(splits[3], (D, KV), 0.02, 0.3125, ((0, 16),), jnp.float32)
    second_moment = jnp.clip(jnp.exp(math.log(1.0) - 2.9957323 * jax.random.uniform(splits[4], (D, KV), jnp.float32) ** block_levels(splits[4], (D, KV), ((0, 16),), -0.2, 0.2)), 0.05, 1.0)
    next_input = normal_values(splits[5], (NEXT_TOKENS, D), 1.0, 6.0, ((0, 256),))
    return {"layer_input": layer_input, "value_cotangent": value_cotangent, "master_weight": master_weight, "first_moment": first_moment, "second_moment": second_moment, "next_input": next_input}


beta_first = 0.9
beta_second = 0.95
learn_rate = 0.001
epsilon = 1e-08

def reference(layer_input, value_cotangent, master_weight, first_moment, second_moment, next_input):
    gradient = lax.dot_general(layer_input, value_cotangent, (((0,), (0,)), ((), ())), preferred_element_type=jnp.float32)
    new_first = beta_first * first_moment + (1.0 - beta_first) * gradient
    new_second = beta_second * second_moment + (1.0 - beta_second) * gradient * gradient
    first_hat = new_first / (1.0 - beta_first ** STEP)
    second_hat = new_second / (1.0 - beta_second ** STEP)
    new_master = master_weight - learn_rate * first_hat / (jnp.sqrt(second_hat) + epsilon)
    weight = new_master.astype(jnp.bfloat16)
    next_values = jnp.dot(next_input, weight, preferred_element_type=jnp.float32).astype(jnp.bfloat16)
    return (new_master, new_first, new_second, next_values)
```

```python
import functools

import jax
import jax.numpy as jnp
from jax import lax
from jax.experimental import pallas as pl
from jax.experimental.pallas import tpu as pltpu
from jax.sharding import PartitionSpec as P

STEP = 200
beta_first = 0.9
beta_second = 0.95
learn_rate = 0.001
epsilon = 1e-08

MESH = pl.DeviceIdType.MESH
BF16 = jnp.bfloat16
F32 = jnp.float32

NX, NY, NZ = 4, 4, 8
AXES = {"x": NX, "y": NY, "z": NZ}
ORDER = (4, 3, 5, 2, 6, 1, 7, 0)
PLACE = {r: k for k, r in enumerate(ORDER)}
UNITS = [(row, col) for row in range(2) for col in range(4)]
STREAM_UNITS = {"x": UNITS[0:3], "y": UNITS[3:6], "z": UNITS[6:8]}


def position():
    cuts, fsdp = lax.axis_index("cuts"), lax.axis_index("fsdp")
    x, y_hi, core = cuts // 4, lax.rem(cuts // 2, 2), lax.rem(cuts, 2)
    z, y_lo = fsdp // 2, lax.rem(fsdp, 2)
    return x, y_hi * 2 + y_lo, z, core


def device(x, y, z, core):
    return (x * 4 + (y // 2) * 2 + core, z * 2 + lax.rem(y, 2))


def kernel(
    x_hbm, c_hbm, master_hbm, first_hbm, second_hbm, next_hbm,
    o_master, o_first, o_second, o_values,
    XB, CB, NB, PX, PY, PZ,
    RXL, RXS, RYL, RYS, RZL, RZS,
    S2X, S2Y, S2Z, R2X, R2Y, R2Z, S3X, S3Y, S3Z, R3X, R3Y, R3Z,
    WX, WY, WZ, GB, MB, FB, SB, WT, VO, VS, VR, VALS,
    load_sem, send_sem, recv_sem, big_send, big_recv,
):
    x, y, z, core = position()
    here = {"x": x, "y": y, "z": z}

    def towards(axis, delta):
        at = dict(here)
        at[axis] = lax.rem(here[axis] + delta, AXES[axis])
        return device(at["x"], at["y"], at["z"], core)

    mate = device(x, y, z, 1 - core)

    counts = {"load": 0, "remote": 0}
    sends = []

    def local(src, dst):
        copy = pltpu.make_async_copy(src, dst, load_sem.at[counts["load"]])
        counts["load"] += 1
        copy.start()
        return copy

    def push(src, dst, dev):
        slot = counts["remote"]
        counts["remote"] += 1
        copy = pltpu.make_async_remote_copy(
            src_ref=src, dst_ref=dst, send_sem=send_sem.at[slot], recv_sem=recv_sem.at[slot],
            device_id=dev, device_id_type=MESH,
        )
        copy.start()
        sends.append(copy)
        return copy

    def block_of(t):
        k = t // 2
        odd = lax.rem(k, 2)
        r = 4 + (1 - odd) * (k // 2) - odd * ((k + 1) // 2)
        return lax.rem(z + r, NZ) * 2 + lax.rem(t, 2)

    def columns(t, side):
        return pl.ds(pl.multiple_of(block_of(t) * 512 + side * 256, 256), 256)

    def x_load(t):
        return pltpu.make_async_copy(
            x_hbm.at[:, columns(t, core)], XB.at[t, pl.ds(0, 512)], big_send.at[32 + t])

    def x_push(t):
        return pltpu.make_async_remote_copy(
            src_ref=x_hbm.at[:, columns(t, 1 - core)], dst_ref=XB.at[t, pl.ds(512, 512)],
            send_sem=big_send.at[t], recv_sem=big_recv.at[t], device_id=mate, device_id_type=MESH)

    def n_load(t):
        return pltpu.make_async_copy(
            next_hbm.at[:, columns(t, core)], NB.at[t, pl.ds(0, 128)], big_send.at[48 + t])

    def n_push(t):
        return pltpu.make_async_remote_copy(
            src_ref=next_hbm.at[:, columns(t, 1 - core)], dst_ref=NB.at[t, pl.ds(128, 128)],
            send_sem=big_send.at[16 + t], recv_sem=big_recv.at[16 + t], device_id=mate, device_id_type=MESH)

    def each(n, act):
        def body(t, carry):
            act(t)
            return carry
        lax.fori_loop(0, n, body, 0)

    c_own = local(c_hbm, CB.at[pl.ds(0, 512)])
    each(16, lambda t: x_load(t).start())

    barrier = pltpu.get_barrier_semaphore()
    partners = [mate] + [towards(a, d) for a in "xyz" for d in range(1, AXES[a])]
    for dev in partners:
        pl.semaphore_signal(barrier, inc=1, device_id=dev, device_id_type=MESH)
    pl.semaphore_wait(barrier, len(partners))

    c_mate = push(c_hbm, CB.at[pl.ds(512, 512)], mate)
    each(16, lambda t: x_push(t).start())
    m_own = local(master_hbm, MB)
    f_own = local(first_hbm, FB)
    s_own = local(second_hbm, SB)
    each(16, lambda t: n_load(t).start())
    each(16, lambda t: n_push(t).start())

    def blocks():
        def make(y_lo):
            out = []
            for g in range(8):
                xa, y_hi = g // 2, g % 2
                xr = lax.rem(xa + NX - x, NX)
                yr = lax.rem(y_hi * 2 + y_lo + NY - y, NY)
                out.append((g, xr, yr))
            return out
        return make

    groups = blocks()

    def tile(t, carry):
        x_load(t).wait()
        x_push(t).wait_recv()
        g_tile = lax.dot_general(
            XB[t], CB[...], (((0,), (0,)), ((), ())), preferred_element_type=F32).astype(BF16)
        k, y_lo = t // 2, lax.rem(t, 2)
        h, kk = k // 4, lax.rem(k, 4)
        for g, xr, yr in groups(y_lo):
            for i, (row, col) in enumerate(STREAM_UNITS["x"]):
                PX[xr, h, yr, kk, i] = g_tile[g * 32 + row * 16:g * 32 + row * 16 + 16, col * 128:col * 128 + 128]
            for i, (row, col) in enumerate(STREAM_UNITS["y"]):
                PY[yr, h, xr, kk, i] = g_tile[g * 32 + row * 16:g * 32 + row * 16 + 16, col * 128:col * 128 + 128]
            for i, (row, col) in enumerate(STREAM_UNITS["z"]):
                PZ[k, xr, yr, i] = g_tile[g * 32 + row * 16:g * 32 + row * 16 + 16, col * 128:col * 128 + 128]
        return carry

    def gemm(first, last):
        lax.fori_loop(first * 2, last * 2, tile, 0)

    def add_rows(dst, terms, n):
        def body(i, carry):
            total = terms[0][i].astype(F32)
            for term in terms[1:]:
                total = total + term[i].astype(F32)
            dst[i] = total.astype(dst.dtype)
            return carry
        lax.fori_loop(0, n, body, 0)

    class Ring:
        def __init__(self, axis, chunk, long_buf, short_buf, rows):
            self.axis, self.chunk, self.long_buf, self.short_buf, self.rows = axis, chunk, long_buf, short_buf, rows
            self.n = AXES[axis]
            self.long, self.short = {}, {}

        def _send(self, way, dist, half, buf, step):
            n = self.n
            r = dist if way == 0 else n - dist
            dev = towards(self.axis, 1 if way == 0 else n - 1)
            return push(self.chunk(r, half), buf.at[way, step], dev)

        def send_long(self, way, step):
            dist = self.n // 2 - step
            if step > 0:
                self.long[way, step - 1].wait_recv()
                r = dist if way == 0 else self.n - dist
                c = self.chunk(r, way)
                add_rows(c, [c, self.long_buf.at[way, step - 1]], self.rows)
            self.long[way, step] = self._send(way, dist, way, self.long_buf, step)

        def send_short(self, way, step):
            dist = self.n // 2 - 1 - step
            if step > 0:
                self.short[way, step - 1].wait_recv()
                r = dist if way == 0 else self.n - dist
                c = self.chunk(r, 1 - way)
                add_rows(c, [c, self.short_buf.at[way, step - 1]], self.rows)
            self.short[way, step] = self._send(way, dist, 1 - way, self.short_buf, step)

        def finish(self):
            n = self.n
            out = []
            for way in range(2):
                self.long[way, n // 2 - 1].wait_recv()
                self.short[way, n // 2 - 2].wait_recv()
            for half in range(2):
                out.append([
                    self.chunk(0, half),
                    self.long_buf.at[half, n // 2 - 1],
                    self.short_buf.at[1 - half, n // 2 - 2],
                ])
            return out

    ring_x = Ring("x", lambda r, h: PX.at[r, h], RXL, RXS, 4)
    ring_y = Ring("y", lambda r, h: PY.at[r, h], RYL, RYS, 4)
    ring_z = Ring("z", lambda r, h: PZ.at[PLACE[r], pl.ds(2 * h, 2)], RZL, RZS, 2)

    c_own.wait()
    c_mate.wait_recv()
    gemm(0, 1)
    ring_z.send_long(0, 0)
    ring_z.send_long(1, 0)
    gemm(1, 3)
    ring_z.send_short(0, 0)
    ring_z.send_short(1, 0)
    gemm(3, 4)
    ring_x.send_long(0, 0)
    ring_y.send_long(0, 0)
    ring_x.send_short(1, 0)
    ring_y.send_short(1, 0)
    ring_z.send_long(0, 1)
    ring_z.send_long(1, 1)
    gemm(4, 8)
    ring_x.send_long(1, 0)
    ring_y.send_long(1, 0)
    ring_x.send_short(0, 0)
    ring_y.send_short(0, 0)
    for way in range(2):
        ring_z.send_short(way, 1)
    for way in range(2):
        ring_z.send_long(way, 2)
    for way in range(2):
        ring_x.send_long(way, 1)
        ring_y.send_long(way, 1)
    for way in range(2):
        ring_z.send_short(way, 2)
    for way in range(2):
        ring_z.send_long(way, 3)

    def spread(axis, src, dst):
        n = AXES[axis]
        far_first = sorted(range(1, n), key=lambda r: -min(r, n - r))
        return [push(src(r), dst(r), towards(axis, r)) for r in far_first]

    def settle(copies):
        for copy in copies:
            copy.wait_recv()

    def ring_total_xy(ring, S):
        for half, terms in enumerate(ring.finish()):
            def body(i, carry, half=half, terms=terms):
                total = terms[0][i].astype(F32) + terms[1][i].astype(F32) + terms[2][i].astype(F32)
                S[i, pl.ds(4 * half, 4)] = total.astype(BF16)
                return carry
            lax.fori_loop(0, 4, body, 0)

    for half, terms in enumerate(ring_z.finish()):
        def body(i, carry, half=half, terms=terms):
            total = terms[0][i].astype(F32) + terms[1][i].astype(F32) + terms[2][i].astype(F32)
            S2Z[2 * half + i] = total.astype(BF16)
            return carry
        lax.fori_loop(0, 2, body, 0)
    z2 = spread("x", lambda r: S2Z.at[r], lambda r: R2Z.at[r - 1])
    ring_total_xy(ring_x, S2X)
    x2 = spread("y", lambda r: S2X.at[r], lambda r: R2X.at[r - 1])
    ring_total_xy(ring_y, S2Y)
    y2 = spread("x", lambda r: S2Y.at[r], lambda r: R2Y.at[r - 1])

    settle(z2)
    add_rows(S3Z, [S2Z.at[0], R2Z.at[0], R2Z.at[1], R2Z.at[2]], 4)
    z3 = spread("y", lambda r: S3Z.at[r], lambda r: R3Z.at[r - 1])
    settle(x2)
    add_rows(S3X, [S2X.at[0], R2X.at[0], R2X.at[1], R2X.at[2]], 8)
    x3 = spread("z", lambda r: S3X.at[PLACE[r]], lambda r: R3X.at[r - 1])
    settle(y2)
    add_rows(S3Y, [S2Y.at[0], R2Y.at[0], R2Y.at[1], R2Y.at[2]], 8)
    y3 = spread("z", lambda r: S3Y.at[PLACE[r]], lambda r: R3Y.at[r - 1])

    m_own.wait()
    f_own.wait()
    s_own.wait()

    def adam(gradient, master, first, second):
        new_first = beta_first * first + (1.0 - beta_first) * gradient
        new_second = beta_second * second + (1.0 - beta_second) * gradient * gradient
        first_hat = new_first / (1.0 - beta_first**STEP)
        second_hat = new_second / (1.0 - beta_second**STEP)
        new_master = master - learn_rate * first_hat / (jnp.sqrt(second_hat) + epsilon)
        return new_master, new_first, new_second

    y_hi = y // 2
    own_row = core * 256 + x * 64 + y_hi * 32

    def own_update(stream, own, received, n, put):
        for i, (row, col) in enumerate(STREAM_UNITS[stream]):
            gradient = own[i].astype(F32)
            for s in range(n):
                gradient = gradient + received[s, i].astype(F32)
            gradient = gradient.astype(BF16)
            GB[0, 0, 0, row * 16:row * 16 + 16, col * 128:col * 128 + 128] = gradient
            rows = pl.ds(pl.multiple_of(own_row + row * 16, 16), 16)
            cols = slice(col * 128, col * 128 + 128)
            new_master, _, _ = adam(gradient.astype(F32), MB[rows, cols], FB[rows, cols], SB[rows, cols])
            put(i, new_master.astype(BF16))

    def put_x(i, w):
        WX[0, 0, 7, i] = w

    def put_y(i, w):
        WY[0, 0, 7, i] = w

    def put_z(i, w):
        WZ[7, 0, 0, i] = w

    settle(z3)
    own_update("z", S3Z.at[0], R3Z, 3, put_z)
    wz1 = spread("y", lambda r: WZ.at[7, 0, 0], lambda r: WZ.at[7, 0, NY - r])
    settle(x3)
    own_update("x", S3X.at[7], R3X, 7, put_x)
    wx1 = spread("z", lambda r: WX.at[0, 0, 7], lambda r: WX.at[0, 0, PLACE[NZ - r]])
    settle(y3)
    own_update("y", S3Y.at[7], R3Y, 7, put_y)
    wy1 = spread("z", lambda r: WY.at[0, 0, 7], lambda r: WY.at[0, 0, PLACE[NZ - r]])
    g1 = spread("x", lambda r: GB.at[0, 0, 0], lambda r: GB.at[0, 0, NX - r])

    settle(wz1)
    wz2 = spread("x", lambda r: WZ.at[7, 0], lambda r: WZ.at[7, NX - r])
    settle(wx1)
    wx2 = spread("y", lambda r: WX.at[0, 0], lambda r: WX.at[0, NY - r])
    settle(wy1)
    wy2 = spread("x", lambda r: WY.at[0, 0], lambda r: WY.at[0, NX - r])

    class Gather:
        def __init__(self, axis, chunk):
            self.axis, self.chunk, self.n = axis, chunk, AXES[axis]
            self.long, self.short = {}, {}

        def _send(self, way, step, half):
            n = self.n
            r = (n - step) % n if way == 0 else step
            land = (n - step - 1) % n if way == 0 else (step + 1) % n
            return push(self.chunk(r, half), self.chunk(land, half), towards(self.axis, 1 if way == 0 else n - 1))

        def send_long(self, way, step):
            if step > 0:
                self.long[way, step - 1].wait_recv()
            self.long[way, step] = self._send(way, step, way)

        def send_short(self, way, step):
            if step > 0:
                self.short[way, step - 1].wait_recv()
            self.short[way, step] = self._send(way, step, 1 - way)

        def finish(self):
            for way in range(2):
                self.long[way, self.n // 2 - 1].wait_recv()
                self.short[way, self.n // 2 - 2].wait_recv()

    gather_x = Gather("x", lambda r, h: WX.at[r, pl.ds(2 * h, 2)])
    gather_y = Gather("y", lambda r, h: WY.at[r, pl.ds(2 * h, 2)])
    gather_z = Gather("z", lambda r, h: WZ.at[PLACE[r], pl.ds(2 * h, 2)])

    settle(wz2)
    for way in range(2):
        gather_z.send_long(way, 0)
        gather_z.send_short(way, 0)
    settle(wx2)
    for way in range(2):
        gather_x.send_long(way, 0)
    for way in range(2):
        gather_x.send_short(way, 0)
    settle(wy2)
    for way in range(2):
        gather_y.send_long(way, 0)
    for way in range(2):
        gather_y.send_short(way, 0)

    settle(g1)
    g2 = push(GB.at[0, 0], GB.at[0, 1], towards("y", 2))

    for way in range(2):
        gather_z.send_long(way, 1)
        gather_z.send_short(way, 1)
    for way in range(2):
        gather_x.send_long(way, 1)
        gather_y.send_long(way, 1)
    for way in range(2):
        gather_z.send_long(way, 2)
        gather_z.send_short(way, 2)
    g2.wait_recv()
    g3 = push(GB.at[0], GB.at[1], mate)
    for way in range(2):
        gather_z.send_long(way, 3)

    def moments(cr):
        def body(i, carry):
            yr, xr = i // 4, lax.rem(i, 4)
            side = core if cr == 0 else 1 - core
            row = side * 256 + lax.rem(x + xr, NX) * 64 + lax.rem(y_hi + yr, 2) * 32
            rows = pl.ds(pl.multiple_of(row, 32), 32)
            new_master, new_first, new_second = adam(
                GB[cr, yr, xr].astype(F32), MB[rows, :], FB[rows, :], SB[rows, :])
            MB[rows, :] = new_master
            FB[rows, :] = new_first
            SB[rows, :] = new_second
            return carry
        lax.fori_loop(0, 8, body, 0)

    moments(0)
    g3.wait_recv()
    moments(1)
    outs = [local(MB, o_master), local(FB, o_first), local(SB, o_second)]

    each(16, lambda t: n_load(t).wait())
    each(16, lambda t: n_push(t).wait_recv())
    gather_z.finish()
    gather_x.finish()
    gather_y.finish()

    VO[...] = jnp.zeros_like(VO)

    def value_tile(t, carry):
        k, y_lo = t // 2, lax.rem(t, 2)
        for g, xr, yr in groups(y_lo):
            def at(row, col):
                return (pl.ds(g * 32 + row * 16, 16), pl.ds(col * 128, 128))
            for i, (row, col) in enumerate(STREAM_UNITS["x"]):
                WT[at(row, col)] = WX[xr, yr, k, i]
            for i, (row, col) in enumerate(STREAM_UNITS["y"]):
                WT[at(row, col)] = WY[yr, xr, k, i]
            for i, (row, col) in enumerate(STREAM_UNITS["z"]):
                WT[at(row, col)] = WZ[k, xr, yr, i]
        VO[...] += jnp.dot(NB[t], WT[...], preferred_element_type=F32)
        return carry

    lax.fori_loop(0, 16, value_tile, 0)
    VS[...] = VO[pl.ds(128, 128), :]
    v_mate = push(VS, VR, mate)
    v_mate.wait_recv()
    VALS[...] = (VO[pl.ds(0, 128), :] + VR[...]).astype(BF16)
    outs.append(local(VALS, o_values))

    for copy in outs:
        copy.wait()
    for copy in sends:
        copy.wait_send()
    each(16, lambda t: x_push(t).wait_send())
    each(16, lambda t: n_push(t).wait_send())


def local_step(layer_input, value_cotangent, master_weight, first_moment, second_moment, next_input):
    unit = (16, 128)
    vm = lambda shape, dtype=BF16: pltpu.VMEM(shape, dtype)
    half_xy = (4, 4, 3) + unit
    half_z = (2, 4, 2) + unit
    scratch = [
        vm((16, 1024, 256)), vm((1024, 512)), vm((16, 256, 256)),
        vm((4, 2, 4, 4, 3) + unit), vm((4, 2, 4, 4, 3) + unit), vm((8, 4, 4, 2) + unit),
        vm((2, 2) + half_xy), vm((2, 1) + half_xy),
        vm((2, 2) + half_xy), vm((2, 1) + half_xy),
        vm((2, 4) + half_z), vm((2, 3) + half_z),
        vm((4, 8, 3) + unit), vm((4, 8, 3) + unit), vm((4, 4, 2) + unit),
        vm((3, 8, 3) + unit), vm((3, 8, 3) + unit), vm((3, 4, 2) + unit),
        vm((8, 3) + unit), vm((8, 3) + unit), vm((4, 2) + unit),
        vm((7, 3) + unit), vm((7, 3) + unit), vm((3, 2) + unit),
        vm((4, 4, 8, 3) + unit), vm((4, 4, 8, 3) + unit), vm((8, 4, 4, 2) + unit),
        vm((2, 2, 4, 32, 512)),
        vm((512, 512), F32), vm((512, 512), F32), vm((512, 512), F32),
        vm((256, 512)), vm((256, 512), F32), vm((128, 512), F32), vm((128, 512), F32), vm((128, 512)),
        pltpu.SemaphoreType.DMA((8,)), pltpu.SemaphoreType.DMA((128,)), pltpu.SemaphoreType.DMA((128,)),
        pltpu.SemaphoreType.DMA((64,)), pltpu.SemaphoreType.DMA((32,)),
    ]
    any_spec = pl.BlockSpec(memory_space=pl.ANY)
    return tuple(pl.pallas_call(
        kernel,
        out_shape=(
            jax.ShapeDtypeStruct((512, 512), F32),
            jax.ShapeDtypeStruct((512, 512), F32),
            jax.ShapeDtypeStruct((512, 512), F32),
            jax.ShapeDtypeStruct((128, 512), BF16),
        ),
        in_specs=[any_spec] * 6,
        out_specs=(any_spec,) * 4,
        scratch_shapes=scratch,
        compiler_params=pltpu.CompilerParams(
            collective_id=0, has_side_effects=True, vmem_limit_bytes=60 * 2**20),
        cost_estimate=pl.CostEstimate(flops=5_400_000_000, bytes_accessed=18_000_000, transcendentals=0),
        name="value_projection_step",
    )(layer_input, value_cotangent, master_weight, first_moment, second_moment, next_input))


def solution(mesh):
    in_specs = (
        P(("cuts", "fsdp"), None),
        P(("cuts", "fsdp"), None),
        P("fsdp", None),
        P("fsdp", None),
        P("fsdp", None),
        P(("cuts", "fsdp"), None),
    )
    out_specs = (P("fsdp", None), P("fsdp", None), P("fsdp", None), P(("cuts", "fsdp"), None))
    return jax.shard_map(local_step, mesh=mesh, in_specs=in_specs, out_specs=out_specs, check_vma=False)
```

```python
import functools

import jax
import jax.numpy as jnp
from jax import lax
from jax.experimental import pallas as pl
from jax.experimental.pallas import tpu as pltpu
from jax.sharding import PartitionSpec as P

STEP = 200
beta_first = 0.9
beta_second = 0.95
learn_rate = 0.001
epsilon = 1e-08

MESH = pl.DeviceIdType.MESH
BF16 = jnp.bfloat16
F32 = jnp.float32

NX, NY, NZ = 4, 4, 8
AXES = {"x": NX, "y": NY, "z": NZ}
ORDER = (4, 3, 5, 2, 6, 1, 7, 0)
PLACE = {r: k for k, r in enumerate(ORDER)}
SLOTS = 232
UNITS = [(row, col) for row in range(2) for col in range(4)]
Q = 4
K = NZ // Q
STREAM_UNITS = {"x": UNITS[0:3], "y": UNITS[3:6], "z": UNITS[6:8]}


def position():
    cuts, fsdp = lax.axis_index("cuts"), lax.axis_index("fsdp")
    x, y_hi, core = cuts // 4, lax.rem(cuts // 2, 2), lax.rem(cuts, 2)
    z, y_lo = fsdp // 2, lax.rem(fsdp, 2)
    return x, y_hi * 2 + y_lo, z, core


def device(x, y, z, core):
    return (x * 4 + (y // 2) * 2 + core, z * 2 + lax.rem(y, 2))


def kernel(
    x_hbm, c_hbm, master_hbm, first_hbm, second_hbm, next_hbm,
    o_master, o_first, o_second, o_values,
    XB, CB, NB, PX, PY, PZ,
    RXL, RXS, RYL, RYS, RZL, RZS,
    S2X, S2Y, S2Z, R2X, R2Y, R2Z, S3X, S3Y, S3Z, R3X, R3Y, R3Z,
    WX, WY, WZ, GB, MB, FB, SB, WT, VO, VS, VR,
    load_sem, send_sem, recv_sem, big_send, big_recv,
):
    x, y, z, core = position()
    here = {"x": x, "y": y, "z": z}

    def towards(axis, delta):
        at = dict(here)
        at[axis] = lax.rem(here[axis] + delta, AXES[axis])
        return device(at["x"], at["y"], at["z"], core)

    mate = device(x, y, z, 1 - core)
    ahead = {(a, d): towards(a, d) for a in "xyz" for d in range(1, AXES[a])}

    barrier = pltpu.get_barrier_semaphore()
    partners = [mate] + [ahead[key] for key in sorted(ahead, key=lambda p: -min(p[1], AXES[p[0]] - p[1]))]
    for dev in partners:
        pl.semaphore_signal(barrier, inc=1, device_id=dev, device_id_type=MESH)

    counts = {"load": 0, "remote": 0}
    sends = []

    def local(src, dst):
        copy = pltpu.make_async_copy(src, dst, load_sem.at[counts["load"]])
        counts["load"] += 1
        copy.start()
        return copy

    class Push:
        def __init__(self, src, dst, dev):
            slot = counts["remote"]
            counts["remote"] += 1
            self.copy = pltpu.make_async_remote_copy(
                src_ref=src, dst_ref=dst, send_sem=send_sem.at[slot], recv_sem=recv_sem.at[slot],
                device_id=dev, device_id_type=MESH,
            )
            self.copy.start()
            self.landed = False
            sends.append(self)

        def arrive(self):
            if not self.landed:
                self.landed = True
                self.copy.wait_recv()

    push = Push

    def block_of(t):
        k = t // 2
        odd = lax.rem(k, 2)
        r = 4 + (1 - odd) * (k // 2) - odd * ((k + 1) // 2)
        return lax.rem(z + r, NZ) * 2 + lax.rem(t, 2)

    def columns(t, side):
        return pl.ds(pl.multiple_of(block_of(t) * 512 + side * 256, 256), 256)

    def x_load(t):
        return pltpu.make_async_copy(
            x_hbm.at[:, columns(t, core)], XB.at[t, pl.ds(0, 512)], big_send.at[32 + t])

    def x_push(t):
        return pltpu.make_async_remote_copy(
            src_ref=x_hbm.at[:, columns(t, 1 - core)], dst_ref=XB.at[t, pl.ds(512, 512)],
            send_sem=big_send.at[t], recv_sem=big_recv.at[t], device_id=mate, device_id_type=MESH)

    def n_place(t, rows):
        return NB.at[t // 4, pl.ds(rows, 128), pl.ds(pl.multiple_of(lax.rem(t, 4) * 256, 256), 256)]

    def n_load(t):
        return pltpu.make_async_copy(next_hbm.at[:, columns(t, core)], n_place(t, 0), big_send.at[48 + t])

    def n_push(t):
        return pltpu.make_async_remote_copy(
            src_ref=next_hbm.at[:, columns(t, 1 - core)], dst_ref=n_place(t, 128),
            send_sem=big_send.at[16 + t], recv_sem=big_recv.at[16 + t], device_id=mate, device_id_type=MESH)

    def each(n, act):
        def body(t, carry):
            act(t)
            return carry
        lax.fori_loop(0, n, body, 0)

    c_own = local(c_hbm, CB.at[pl.ds(0, 512)])
    each(16, lambda t: x_load(t).start())
    pl.semaphore_wait(barrier, len(partners))

    c_mate = push(c_hbm, CB.at[pl.ds(512, 512)], mate)
    each(16, lambda t: x_push(t).start())
    m_own = local(master_hbm, MB)
    f_own = local(first_hbm, FB)
    s_own = local(second_hbm, SB)
    each(16, lambda t: n_load(t).start())
    each(16, lambda t: n_push(t).start())

    def groups(y_lo):
        out = []
        for g in range(8):
            xr = lax.rem(g // 2 + NX - x, NX)
            yr = lax.rem((g % 2) * 2 + y_lo + NY - y, NY)
            out.append((g, xr, yr))
        return out

    def tile(t, carry):
        x_load(t).wait()
        x_push(t).wait_recv()
        g_tile = lax.dot_general(
            XB[t], CB[...], (((0,), (0,)), ((), ())), preferred_element_type=F32).astype(BF16)
        k, y_lo = t // 2, lax.rem(t, 2)
        q, kk = k // K, lax.rem(k, K)

        def piece(g, unit):
            row, col = unit
            return g_tile[g * 32 + row * 16:g * 32 + row * 16 + 16, col * 128:col * 128 + 128]

        for g, xr, yr in groups(y_lo):
            for i, unit in enumerate(STREAM_UNITS["x"]):
                PX[xr, q, yr, kk, i] = piece(g, unit)
            for i, unit in enumerate(STREAM_UNITS["y"]):
                PY[yr, q, xr, kk, i] = piece(g, unit)
            for i, unit in enumerate(STREAM_UNITS["z"]):
                PZ[k, xr, yr, i] = piece(g, unit)
        return carry

    def gemm(first, last):
        lax.fori_loop(first * 2, last * 2, tile, 0)

    def add_rows(dst, terms, n):
        def body(i, carry):
            total = terms[0][i].astype(F32)
            for term in terms[1:]:
                total = total + term[i].astype(F32)
            dst[i] = total.astype(dst.dtype)
            return carry
        lax.fori_loop(0, n, body, 0)

    class Ring:
        def __init__(self, axis, chunk, long_buf, short_buf, rows):
            self.axis, self.chunk, self.long_buf, self.short_buf, self.rows = axis, chunk, long_buf, short_buf, rows
            self.n = AXES[axis]
            self.long, self.short = {}, {}

        def _send(self, copies, buf, way, step, dist, half):
            n = self.n
            chunk = self.chunk(dist if way == 0 else n - dist, half)
            if step > 0:
                copies[way, step - 1].arrive()
                add_rows(chunk, [chunk, buf.at[way, step - 1]], self.rows)
            copies[way, step] = push(chunk, buf.at[way, step], ahead[self.axis, 1 if way == 0 else n - 1])

        def send_long(self, way, step):
            self._send(self.long, self.long_buf, way, step, self.n // 2 - step, way)

        def send_short(self, way, step):
            self._send(self.short, self.short_buf, way, step, self.n // 2 - 1 - step, 1 - way)

        def total(self, dst):
            n = self.n
            for way in range(2):
                self.short[way, n // 2 - 2].arrive()
                self.long[way, n // 2 - 1].arrive()
            for half in range(2):
                add_rows(dst(half), [
                    self.chunk(0, half),
                    self.long_buf.at[half, n // 2 - 1],
                    self.short_buf.at[1 - half, n // 2 - 2],
                ], self.rows)

    def spread(axis, src, dst, order):
        return {r: push(src(r), dst(r), ahead[axis, r]) for r in order}

    def settle(copies):
        for copy in copies.values():
            copy.arrive()

    ring_x = [Ring("x", lambda r, h, q=q: PX.at[r, q, pl.ds(2 * h, 2)], RXL.at[q], RXS.at[q], 2) for q in range(Q)]
    ring_y = [Ring("y", lambda r, h, q=q: PY.at[r, q, pl.ds(2 * h, 2)], RYL.at[q], RYS.at[q], 2) for q in range(Q)]
    ring_z = Ring("z", lambda r, h: PZ.at[PLACE[r], pl.ds(2 * h, 2)], RZL, RZS, 2)

    second_x, second_y, third_x, third_y = {}, {}, {}, {}

    def first_hops(q):
        for way in range(2):
            ring_x[q].send_long(way, 0)
            ring_y[q].send_long(way, 0)
        for way in range(2):
            ring_x[q].send_short(way, 0)
            ring_y[q].send_short(way, 0)

    def last_hops(q):
        for way in range(2):
            ring_x[q].send_long(way, 1)
            ring_y[q].send_long(way, 1)

    def second(q):
        ring_x[q].total(lambda half: S2X.at[q, pl.ds(2 * half, 2)])
        second_x[q] = spread("y", lambda r: S2X.at[q, r], lambda r: R2X.at[q, r - 1], (2, 1, 3))
        ring_y[q].total(lambda half: S2Y.at[q, pl.ds(2 * half, 2)])
        second_y[q] = spread("x", lambda r: S2Y.at[q, r], lambda r: R2Y.at[q, r - 1], (2, 1, 3))

    def third(q):
        order = [r for r in ORDER[K * q:K * q + K] if r > 0]
        settle(second_x[q])
        add_rows(S3X.at[pl.ds(K * q, K)], [S2X.at[q, 0]] + [R2X.at[q, r] for r in range(3)], K)
        third_x.update(spread("z", lambda r: S3X.at[PLACE[r]], lambda r: R3X.at[r - 1], order))
        settle(second_y[q])
        add_rows(S3Y.at[pl.ds(K * q, K)], [S2Y.at[q, 0]] + [R2Y.at[q, r] for r in range(3)], K)
        third_y.update(spread("z", lambda r: S3Y.at[PLACE[r]], lambda r: R3Y.at[r - 1], order))

    def z_long(step):
        for way in range(2):
            ring_z.send_long(way, step)

    def z_short(step):
        for way in range(2):
            ring_z.send_short(way, step)

    c_own.wait()
    c_mate.arrive()
    gemm(0, 1)
    z_long(0)
    gemm(1, 2)
    first_hops(0)
    gemm(2, 3)
    z_short(0)
    gemm(3, 4)
    first_hops(1)
    z_long(1)
    gemm(4, 6)
    first_hops(2)
    last_hops(0)
    z_short(1)
    z_long(2)
    gemm(6, 8)
    first_hops(3)
    last_hops(1)
    second(0)
    z_short(2)
    z_long(3)
    last_hops(2)
    second(1)
    third(0)
    last_hops(3)
    second(2)
    third(1)
    ring_z.total(lambda half: S2Z.at[pl.ds(2 * half, 2)])
    second_z = spread("x", lambda r: S2Z.at[r], lambda r: R2Z.at[r - 1], (2, 1, 3))
    second(3)
    third(2)
    settle(second_z)
    add_rows(S3Z, [S2Z.at[0], R2Z.at[0], R2Z.at[1], R2Z.at[2]], 4)
    third_z = spread("y", lambda r: S3Z.at[r], lambda r: R3Z.at[r - 1], (2, 1, 3))
    third(3)

    m_own.wait()
    f_own.wait()
    s_own.wait()

    def adam(gradient, master, first, second):
        new_first = beta_first * first + (1.0 - beta_first) * gradient
        new_second = beta_second * second + (1.0 - beta_second) * gradient * gradient
        first_hat = new_first / (1.0 - beta_first**STEP)
        second_hat = new_second / (1.0 - beta_second**STEP)
        new_master = master - learn_rate * first_hat / (jnp.sqrt(second_hat) + epsilon)
        return new_master, new_first, new_second

    y_hi = y // 2
    own_row = core * 256 + x * 64 + y_hi * 32

    def own_update(stream, own, received, n, dst):
        for i, (row, col) in enumerate(STREAM_UNITS[stream]):
            gradient = own[i].astype(F32)
            for s in range(n):
                gradient = gradient + received[s, i].astype(F32)
            gradient = gradient.astype(BF16)
            GB[0, 0, 0, row * 16:row * 16 + 16, col * 128:col * 128 + 128] = gradient
            rows = pl.ds(pl.multiple_of(own_row + row * 16, 16), 16)
            cols = slice(col * 128, col * 128 + 128)
            new_master, _, _ = adam(gradient.astype(F32), MB[rows, cols], FB[rows, cols], SB[rows, cols])
            dst[i] = new_master.astype(BF16)

    def slot(k):
        return k // K, k % K

    def w_x(k):
        q, kk = slot(k)
        return WX.at[0, q, 0, kk]

    def w_y(k):
        q, kk = slot(k)
        return WY.at[0, q, 0, kk]

    near_first = (1, 7, 2, 6, 3, 5, 4)
    settle(third_z)
    own_update("z", S3Z.at[0], R3Z, 3, WZ.at[7, 0, 0])
    wz1 = spread("y", lambda r: WZ.at[7, 0, 0], lambda r: WZ.at[7, 0, NY - r], (2, 1, 3))
    settle(third_x)
    own_update("x", S3X.at[7], R3X, 7, w_x(7))
    wx1 = spread("z", lambda r: w_x(7), lambda r: w_x(PLACE[NZ - r]), near_first)
    settle(third_y)
    own_update("y", S3Y.at[7], R3Y, 7, w_y(7))
    wy1 = spread("z", lambda r: w_y(7), lambda r: w_y(PLACE[NZ - r]), near_first)
    g1 = spread("x", lambda r: GB.at[0, 0, 0], lambda r: GB.at[0, 0, NX - r], (2, 1, 3))

    class Gather:
        def __init__(self, axis, chunk):
            self.axis, self.chunk, self.n = axis, chunk, AXES[axis]
            self.long, self.short = {}, {}

        def _send(self, copies, way, step, half):
            n = self.n
            if step > 0:
                copies[way, step - 1].arrive()
            r = (n - step) % n if way == 0 else step
            land = (n - step - 1) % n if way == 0 else (step + 1) % n
            copies[way, step] = push(
                self.chunk(r, half), self.chunk(land, half), ahead[self.axis, 1 if way == 0 else n - 1])

        def send_long(self, way, step):
            self._send(self.long, way, step, way)

        def send_short(self, way, step):
            self._send(self.short, way, step, 1 - way)

        def finish(self):
            settle(self.short)
            settle(self.long)

    gather_x = [Gather("x", lambda r, h, q=q: WX.at[r, q, pl.ds(2 * h, 2)]) for q in range(Q)]
    gather_y = [Gather("y", lambda r, h, q=q: WY.at[r, q, pl.ds(2 * h, 2)]) for q in range(Q)]
    gather_z = Gather("z", lambda r, h: WZ.at[PLACE[r], pl.ds(2 * h, 2)])

    across_x, across_y = {}, {}

    def across(q):
        near = [NZ - r for r in ORDER[K * q:K * q + K] if r > 0]
        for r in near:
            wx1[r].arrive()
        across_x[q] = spread("y", lambda r: WX.at[0, q, 0], lambda r: WX.at[0, q, NY - r], (2, 1, 3))
        for r in near:
            wy1[r].arrive()
        across_y[q] = spread("x", lambda r: WY.at[0, q, 0], lambda r: WY.at[0, q, NX - r], (2, 1, 3))

    def go_round(q):
        settle(across_x[q])
        for way in range(2):
            gather_x[q].send_long(way, 0)
        settle(across_y[q])
        for way in range(2):
            gather_y[q].send_long(way, 0)
        for way in range(2):
            gather_x[q].send_short(way, 0)
            gather_y[q].send_short(way, 0)

    def go_on(q):
        for way in range(2):
            gather_x[q].send_long(way, 1)
            gather_y[q].send_long(way, 1)

    def z_gather(step):
        for way in range(2):
            gather_z.send_long(way, step)
            if step < 3:
                gather_z.send_short(way, step)

    def moments(cr):
        def body(i, carry):
            yr, xr = i // 4, lax.rem(i, 4)
            side = core if cr == 0 else 1 - core
            row = side * 256 + lax.rem(x + xr, NX) * 64 + lax.rem(y_hi + yr, 2) * 32
            rows = pl.ds(pl.multiple_of(row, 32), 32)
            new_master, new_first, new_second = adam(
                GB[cr, yr, xr].astype(F32), MB[rows, :], FB[rows, :], SB[rows, :])
            o_master[rows, :] = new_master
            o_first[rows, :] = new_first
            o_second[rows, :] = new_second
            return carry
        lax.fori_loop(0, 8, body, 0)

    def values(q):
        gather_x[q].finish()
        gather_y[q].finish()
        for r in ORDER[K * q:K * q + K]:
            for way in range(2):
                dist = NZ - r if way == 0 else r
                for half, copies in ((way, gather_z.long), (1 - way, gather_z.short)):
                    if (way, dist - 1) in copies:
                        copies[way, dist - 1].arrive()

        def body(j, carry):
            kk, y_lo = j // 2, lax.rem(j, 2)
            for g, xr, yr in groups(y_lo):
                def put(unit, w):
                    row, col = unit
                    at = pl.ds(pl.multiple_of(j * 256 + g * 32 + row * 16, 16), 16)
                    WT[at, col * 128:col * 128 + 128] = w
                for i, unit in enumerate(STREAM_UNITS["x"]):
                    put(unit, WX[xr, q, yr, kk, i])
                for i, unit in enumerate(STREAM_UNITS["y"]):
                    put(unit, WY[yr, q, xr, kk, i])
                for i, unit in enumerate(STREAM_UNITS["z"]):
                    put(unit, WZ[K * q + kk, xr, yr, i])
            return carry
        lax.fori_loop(0, 2 * K, body, 0)
        product = jnp.dot(NB[q], WT[...], preferred_element_type=F32)
        if q == Q - 1:
            VO[...] = product
        else:
            VO[...] += product

    settle(wz1)
    wz2 = spread("x", lambda r: WZ.at[7, 0], lambda r: WZ.at[7, NX - r], (2, 1, 3))
    across(3)
    across(2)
    settle(wz2)
    z_gather(0)
    go_round(3)
    across(1)
    go_round(2)
    across(0)
    settle(g1)
    g2 = push(GB.at[0, 0], GB.at[0, 1], ahead["y", 2])
    z_gather(1)
    go_on(3)
    go_round(1)
    go_on(2)
    z_gather(2)
    go_round(0)
    g2.arrive()
    g3 = push(GB.at[0], GB.at[1], mate)
    go_on(1)
    z_gather(3)
    each(16, lambda t: n_load(t).wait())
    each(16, lambda t: n_push(t).wait_recv())
    moments(0)
    values(3)
    go_on(0)
    g3.arrive()
    moments(1)
    values(2)
    values(1)
    values(0)
    VS[...] = VO[pl.ds(128, 128), :]
    v_mate = push(VS, VR, mate)
    v_mate.arrive()
    o_values[...] = (VO[pl.ds(0, 128), :] + VR[...]).astype(BF16)

    for sent in sends:
        sent.copy.wait_send()
    each(16, lambda t: x_push(t).wait_send())
    each(16, lambda t: n_push(t).wait_send())


def place(a, b, c, d, o_a, o_b, o_c, o_d, sem):
    copies = [
        pltpu.make_async_copy(src, dst, sem.at[i])
        for i, (src, dst) in enumerate(((a, o_a), (b, o_b), (c, o_c), (d, o_d)))
    ]
    for copy in copies:
        copy.start()
    for copy in copies:
        copy.wait()


OUTS = (((512, 512), F32), ((512, 512), F32), ((512, 512), F32), ((128, 512), BF16))


def local_step(layer_input, value_cotangent, master_weight, first_moment, second_moment, next_input):
    unit = (16, 128)

    def vm(*shape, dtype=BF16):
        return pltpu.VMEM(shape, dtype)

    half_xy = (2, K, 3) + unit
    half_z = (2, 4, 2) + unit
    scratch = [
        vm(16, 1024, 256), vm(1024, 512), vm(Q, 256, 1024),
        vm(4, Q, 4, K, 3, *unit), vm(4, Q, 4, K, 3, *unit), vm(8, 4, 4, 2, *unit),
        vm(Q, 2, 2, *half_xy), vm(Q, 2, 1, *half_xy),
        vm(Q, 2, 2, *half_xy), vm(Q, 2, 1, *half_xy),
        vm(2, 4, *half_z), vm(2, 3, *half_z),
        vm(Q, 4, K, 3, *unit), vm(Q, 4, K, 3, *unit), vm(4, 4, 2, *unit),
        vm(Q, 3, K, 3, *unit), vm(Q, 3, K, 3, *unit), vm(3, 4, 2, *unit),
        vm(8, 3, *unit), vm(8, 3, *unit), vm(4, 2, *unit),
        vm(7, 3, *unit), vm(7, 3, *unit), vm(3, 2, *unit),
        vm(4, Q, 4, K, 3, *unit), vm(4, Q, 4, K, 3, *unit), vm(8, 4, 4, 2, *unit),
        vm(2, 2, 4, 32, 512),
        vm(512, 512, dtype=F32), vm(512, 512, dtype=F32), vm(512, 512, dtype=F32),
        vm(1024, 512), vm(256, 512, dtype=F32), vm(128, 512, dtype=F32), vm(128, 512, dtype=F32),
        pltpu.SemaphoreType.DMA((4,)), pltpu.SemaphoreType.DMA((SLOTS,)), pltpu.SemaphoreType.DMA((SLOTS,)),
        pltpu.SemaphoreType.DMA((64,)), pltpu.SemaphoreType.DMA((32,)),
    ]
    results = pl.pallas_call(
        kernel,
        out_shape=tuple(pltpu.VMEM(shape, dtype) for shape, dtype in OUTS),
        in_specs=[pl.BlockSpec(memory_space=pl.ANY)] * 6,
        out_specs=(pl.BlockSpec(memory_space=pltpu.VMEM),) * 4,
        scratch_shapes=scratch,
        compiler_params=pltpu.CompilerParams(
            collective_id=0, has_side_effects=True, vmem_limit_bytes=56 * 2**20),
        cost_estimate=pl.CostEstimate(flops=5_400_000_000, bytes_accessed=18_000_000, transcendentals=0),
        name="value_projection_step",
    )(layer_input, value_cotangent, master_weight, first_moment, second_moment, next_input)
    return tuple(pl.pallas_call(
        place,
        out_shape=tuple(jax.ShapeDtypeStruct(shape, dtype) for shape, dtype in OUTS),
        in_specs=[pl.BlockSpec(memory_space=pltpu.VMEM)] * 4,
        out_specs=(pl.BlockSpec(memory_space=pl.ANY),) * 4,
        scratch_shapes=[pltpu.SemaphoreType.DMA((4,))],
        compiler_params=pltpu.CompilerParams(vmem_limit_bytes=2**20),
        name="place_results",
    )(*results))


def solution(mesh):
    in_specs = (
        P(("cuts", "fsdp"), None),
        P(("cuts", "fsdp"), None),
        P("fsdp", None),
        P("fsdp", None),
        P("fsdp", None),
        P(("cuts", "fsdp"), None),
    )
    out_specs = (P("fsdp", None), P("fsdp", None), P("fsdp", None), P(("cuts", "fsdp"), None))
    return jax.shard_map(local_step, mesh=mesh, in_specs=in_specs, out_specs=out_specs, check_vma=False)
```

```python
import functools

import jax
import jax.numpy as jnp
from jax import lax
from jax.experimental import pallas as pl
from jax.experimental.pallas import tpu as pltpu
from jax.sharding import PartitionSpec as P

STEP = 200
beta_first = 0.9
beta_second = 0.95
learn_rate = 0.001
epsilon = 1e-08

MESH = pl.DeviceIdType.MESH
BF16 = jnp.bfloat16
F32 = jnp.float32

NX, NY, NZ = 4, 4, 8
POOL = 24
ARRIVALS = 80
AXES = {"x": NX, "y": NY, "z": NZ}
ORDER = (4, 3, 5, 2, 6, 1, 7, 0)
PLACE = {r: k for k, r in enumerate(ORDER)}
Q = 4
K = NZ // Q
PARTS = 4
STREAMS = {
    "x": ("x", "y", [(0, 0), (0, 1), (0, 2)]),
    "y": ("y", "x", [(0, 3), (1, 0), (1, 1)]),
}
Z_UNITS = [(1, 2), (1, 3)]


def position():
    cuts, fsdp = lax.axis_index("cuts"), lax.axis_index("fsdp")
    x, y_hi, core = cuts // 4, lax.rem(cuts // 2, 2), lax.rem(cuts, 2)
    z, y_lo = fsdp // 2, lax.rem(fsdp, 2)
    return x, y_hi * 2 + y_lo, z, core


def device(x, y, z, core):
    return (x * 4 + (y // 2) * 2 + core, z * 2 + lax.rem(y, 2))


def kernel(
    x_hbm, c_hbm, master_hbm, first_hbm, second_hbm, next_hbm,
    o_master, o_first, o_second, o_values,
    XB, CB, NB, PZ, RZL, RZS, S2Z, R2Z, S3Z, R3Z, WZ,
    buf_x, buf_y,
    GB, MFS, WT, VO, VS, VR,
    send_sem, recv_sem, x_sem, bulk_sem,
):
    x, y, z, core = position()
    here = {"x": x, "y": y, "z": z}

    def towards(axis, delta):
        at = dict(here)
        at[axis] = lax.rem(here[axis] + delta, AXES[axis])
        return device(at["x"], at["y"], at["z"], core)

    mate = device(x, y, z, 1 - core)
    ahead = {(a, d): towards(a, d) for a in "xyz" for d in range(1, AXES[a])}

    barrier = pltpu.get_barrier_semaphore()
    partners = [mate] + [ahead[key] for key in sorted(ahead, key=lambda p: -min(p[1], AXES[p[0]] - p[1]))]
    for dev in partners:
        pl.semaphore_signal(barrier, inc=1, device_id=dev, device_id_type=MESH)

    counts = {"arrival": 0, "group": 0}
    pool = [None] * POOL

    def arrival():
        counts["arrival"] += 1
        return recv_sem.at[counts["arrival"] - 1]

    def wait_bytes(ref, sem):
        pltpu.make_async_copy(ref, ref, sem).wait()

    class Group:
        def __init__(self, items, whole, recv=None):
            slot = counts["group"] % POOL
            counts["group"] += 1
            if pool[slot] is not None:
                pool[slot].leave()
            pool[slot] = self
            self.whole, self.sem = whole, send_sem.at[slot]
            self.recv = arrival() if recv is None else None
            self.landed = recv is not None
            for i, (src, dst, dev) in enumerate(items):
                sem = self.recv if recv is None else recv[i] if isinstance(recv, list) else recv
                pltpu.make_async_remote_copy(
                    src_ref=src, dst_ref=dst, send_sem=self.sem, recv_sem=sem,
                    device_id=dev, device_id_type=MESH,
                ).start()

        def leave(self):
            wait_bytes(self.whole, self.sem)

        def arrive(self):
            if not self.landed:
                self.landed = True
                wait_bytes(self.whole, self.recv)

    def block_of(t):
        k = t // 2
        odd = lax.rem(k, 2)
        r = 4 + (1 - odd) * (k // 2) - odd * ((k + 1) // 2)
        return lax.rem(z + r, NZ) * 2 + lax.rem(t, 2)

    def columns(t, side):
        return pl.ds(pl.multiple_of(block_of(t) * 512 + side * 256, 256), 256)

    def x_load(t):
        return pltpu.make_async_copy(
            x_hbm.at[:, columns(t, core)], XB.at[t, pl.ds(0, 512)], x_sem.at[t])

    def x_push(t):
        return pltpu.make_async_remote_copy(
            src_ref=x_hbm.at[:, columns(t, 1 - core)], dst_ref=XB.at[t, pl.ds(512, 512)],
            send_sem=bulk_sem.at[0], recv_sem=x_sem.at[t], device_id=mate, device_id_type=MESH)

    def n_place(t, rows):
        return NB.at[t // 4, pl.ds(rows, 128), pl.ds(pl.multiple_of(lax.rem(t, 4) * 256, 256), 256)]

    def n_load(t):
        return pltpu.make_async_copy(next_hbm.at[:, columns(t, core)], n_place(t, 0), bulk_sem.at[2])

    def n_push(t):
        return pltpu.make_async_remote_copy(
            src_ref=next_hbm.at[:, columns(t, 1 - core)], dst_ref=n_place(t, 128),
            send_sem=bulk_sem.at[1], recv_sem=bulk_sem.at[2], device_id=mate, device_id_type=MESH)

    def each(n, act):
        def body(t, carry):
            act(t)
            return carry
        lax.fori_loop(0, n, body, 0)

    c_sem = arrival()
    pltpu.make_async_copy(c_hbm, CB.at[pl.ds(0, 512)], c_sem).start()
    each(16, lambda t: x_load(t).start())
    pl.semaphore_wait(barrier, len(partners))

    Group([(c_hbm, CB.at[pl.ds(512, 512)], mate)], CB.at[pl.ds(512, 512)], c_sem)
    each(16, lambda t: x_push(t).start())
    for i, ref in enumerate((master_hbm, first_hbm, second_hbm)):
        pltpu.make_async_copy(ref, MFS.at[i], bulk_sem.at[3]).start()
    each(16, lambda t: n_load(t).start())
    each(16, lambda t: n_push(t).start())

    def groups(y_lo):
        out = []
        for g in range(8):
            xr = lax.rem(g // 2 + NX - x, NX)
            yr = lax.rem((g % 2) * 2 + y_lo + NY - y, NY)
            out.append((g, xr, yr))
        return out

    def tile(t, carry):
        wait_bytes(XB.at[t], x_sem.at[t])
        g_tile = lax.dot_general(
            XB[t], CB[...], (((0,), (0,)), ((), ())), preferred_element_type=F32).astype(BF16)
        k, y_lo = t // 2, lax.rem(t, 2)
        q, kk = k // K, lax.rem(k, K)

        def piece(g, unit):
            row, col = unit
            return g_tile[g * 32 + row * 16:g * 32 + row * 16 + 16, col * 128:col * 128 + 128]

        for g, xr, yr in groups(y_lo):
            for st in streams.values():
                for i, unit in enumerate(st.units):
                    st.P[st.places(xr, q, yr, kk, i)] = piece(g, unit)
            for i, unit in enumerate(Z_UNITS):
                PZ[k, xr, yr, i] = piece(g, unit)
        return carry

    def gemm(first, last):
        lax.fori_loop(first * 2, last * 2, tile, 0)

    def add_rows(dst, terms, n):
        def body(i, carry):
            total = terms[0][i].astype(F32)
            for term in terms[1:]:
                total = total + term[i].astype(F32)
            dst[i] = total.astype(dst.dtype)
            return carry
        lax.fori_loop(0, n, body, 0)

    def both_ways(axis):
        return ahead[axis, 1], ahead[axis, AXES[axis] - 1]

    class Ring:
        def __init__(self, axis, chunk, long_buf, short_buf, rows):
            self.axis, self.chunk, self.long_buf, self.short_buf, self.rows = axis, chunk, long_buf, short_buf, rows
            self.n = AXES[axis]
            self.long, self.short, self.last = {}, {}, None

        def _send(self, copies, buf, step, dist, halves, recv=None):
            chunks = [self.chunk(dist, halves[0]), self.chunk(self.n - dist, halves[1])]
            if step > 0:
                copies[step - 1].arrive()
                for way in range(2):
                    add_rows(chunks[way], [chunks[way], buf.at[step - 1, way]], self.rows)
            devs = both_ways(self.axis)
            copies[step] = Group([(chunks[w], buf.at[step, w], devs[w]) for w in range(2)], buf.at[step], recv)

        def send_long(self, step, recv=None):
            self._send(self.long, self.long_buf, step, self.n // 2 - step, (0, 1), recv)

        def send_short(self, step, recv=None):
            self._send(self.short, self.short_buf, step, self.n // 2 - 1 - step, (1, 0), recv)

        def total(self, dst):
            n = self.n
            for half in range(2):
                add_rows(dst(half), [
                    self.chunk(0, half),
                    self.long_buf.at[n // 2 - 1, half],
                    self.short_buf.at[n // 2 - 2, 1 - half],
                ], self.rows)

    def spread(axis, src, dst, order, whole, recv=None):
        return Group([(src(r), dst(r), ahead[axis, r]) for r in order], whole, recv)

    ring_z = Ring("z", lambda r, h: PZ.at[PLACE[r], pl.ds(2 * h, 2)], RZL, RZS, 2)

    def z_long(step):
        ring_z.send_long(step)

    def z_short(step):
        ring_z.send_short(step)

    def adam(gradient, master, first, second):
        new_first = beta_first * first + (1.0 - beta_first) * gradient
        new_second = beta_second * second + (1.0 - beta_second) * gradient * gradient
        first_hat = new_first / (1.0 - beta_first**STEP)
        second_hat = new_second / (1.0 - beta_second**STEP)
        new_master = master - learn_rate * first_hat / (jnp.sqrt(second_hat) + epsilon)
        return new_master, new_first, new_second

    y_hi = y // 2
    own_row = core * 256 + x * 64 + y_hi * 32

    def own_update(units, own, received, n, dst):
        for n_unit, (row, col) in enumerate(units):
            gradient = own[n_unit].astype(F32)
            for s in range(n):
                gradient = gradient + received[s, n_unit].astype(F32)
            gradient = gradient.astype(BF16)
            GB[0, 0, 0, row * 16:row * 16 + 16, col * 128:col * 128 + 128] = gradient
            rows = pl.ds(pl.multiple_of(own_row + row * 16, 16), 16)
            cols = slice(col * 128, col * 128 + 128)
            new_master, _, _ = adam(gradient.astype(F32), *(MFS[i, rows, cols] for i in range(3)))
            dst[n_unit] = new_master.astype(BF16)

    near_first = (1, 7, 2, 6, 3, 5, 4)

    class Stream:
        def __init__(self, name, bufs):
            self.axis, self.other, self.units = STREAMS[name]
            self.P, self.RL, self.RS, self.S2, self.R2, self.S3, self.R3, self.W = bufs
            self.two, self.near, self.across_, self.long = {}, {}, {}, {}
            self.ring_last = [arrival() for _ in range(Q)]
            self.gather_last = [arrival() for _ in range(Q)]
            self.back = [arrival() for _ in range(Q)]
            self.three = arrival()

        def half(self, r, q, h):
            return self.P.at[r, q, pl.ds(2 * h, 2)]

        def part(self, r, q, h):
            return self.W.at[r, q, pl.ds(2 * h, 2)]

        def places(self, xr, q, yr, kk, i):
            return (xr, q, yr, kk, i) if self.axis == "x" else (yr, q, xr, kk, i)

        def hop0(self, q):
            devs = both_ways(self.axis)
            self.near[q] = Group(
                [(self.half(2, q, w), self.RL.at[q, w], devs[w]) for w in range(2)], self.RL.at[q])
            Group(
                [(self.half(1 + 2 * w, q, 1 - w), self.RS.at[q, 2 + w], devs[w]) for w in range(2)],
                self.RL.at[q], self.ring_last[q])

        def hop1(self, q):
            devs = both_ways(self.axis)
            self.near[q].arrive()
            for w in range(2):
                chunk = self.half(1 + 2 * w, q, w)
                add_rows(chunk, [chunk, self.RL.at[q, w]], 2)
            Group(
                [(self.half(1 + 2 * w, q, w), self.RS.at[q, w], devs[w]) for w in range(2)],
                self.RL.at[q], self.ring_last[q])

        def second(self, q):
            wait_bytes(self.RS.at[q], self.ring_last[q])
            for h in range(2):
                add_rows(
                    self.S2.at[q, pl.ds(2 * h, 2)], [self.half(0, q, h), self.RS.at[q, h], self.RS.at[q, 3 - h]], 2)
            self.two[q] = spread(
                self.other, lambda r: self.S2.at[q, r], lambda r: self.R2.at[q, r - 1], (2, 1, 3), self.R2.at[q])

        def third(self, q):
            self.two[q].arrive()
            add_rows(self.S3.at[pl.ds(K * q, K)], [self.S2.at[q, 0]] + [self.R2.at[q, r] for r in range(3)], K)
            order = [r for r in ORDER[K * q:K * q + K] if r > 0]
            spread("z", lambda r: self.S3.at[PLACE[r]], lambda r: self.R3.at[r - 1], order,
                   self.S3.at[pl.ds(K * q, len(order))], self.three)

        def own(self, r):
            return self.W.at[0, PLACE[r] // K, 0, PLACE[r] % K]

        def update(self):
            wait_bytes(self.R3, self.three)
            own_update(self.units, self.S3.at[7], self.R3, 7, self.own(0))
            spread("z", lambda r: self.own(0), lambda r: self.own(NZ - r), near_first, self.R3,
                   [self.back[PLACE[NZ - r] // K] for r in near_first])

        def across(self, q):
            came = len([r for r in ORDER[K * q:K * q + K] if r > 0])
            wait_bytes(self.W.at[0, q, 0, pl.ds(0, came)], self.back[q])
            self.across_[q] = spread(
                self.other, lambda r: self.W.at[0, q, 0], lambda r: self.W.at[0, q, 4 - r], (2, 1, 3),
                self.W.at[0, q, pl.ds(1, 3)])

        def go0(self, q):
            devs = both_ways(self.axis)
            self.across_[q].arrive()
            self.long[q] = Group(
                [(self.part(0, q, w), self.part(3 - 2 * w, q, w), devs[w]) for w in range(2)], self.W.at[0, q])
            Group(
                [(self.part(0, q, 1 - w), self.part(3 - 2 * w, q, 1 - w), devs[w]) for w in range(2)],
                self.W.at[0, q], self.gather_last[q])

        def go1(self, q):
            devs = both_ways(self.axis)
            self.long[q].arrive()
            Group(
                [(self.part(3 - 2 * w, q, w), self.part(2, q, w), devs[w]) for w in range(2)],
                self.W.at[0, q], self.gather_last[q])

        def finish(self, q):
            wait_bytes(self.W.at[pl.ds(0, 2), q], self.gather_last[q])

    streams = {name: Stream(name, bufs) for name, bufs in zip(STREAMS, (buf_x, buf_y))}
    x_s, y_s = streams.values()
    zs = {}

    def z_second():
        ring_z.long[3].arrive()
        ring_z.short[2].arrive()
        ring_z.total(lambda half: S2Z.at[pl.ds(2 * half, 2)])
        zs["two"] = spread("x", lambda r: S2Z.at[r], lambda r: R2Z.at[r - 1], (2, 1, 3), R2Z)

    def z_third():
        zs["two"].arrive()
        add_rows(S3Z, [S2Z.at[0], R2Z.at[0], R2Z.at[1], R2Z.at[2]], 4)
        zs["three"] = spread("y", lambda r: S3Z.at[r], lambda r: R3Z.at[r - 1], (2, 1, 3), R3Z)

    def z_update():
        zs["three"].arrive()
        own_update(Z_UNITS, S3Z.at[0], R3Z, 3, WZ.at[7, 0, 0])
        zs["back_y"] = spread(
            "y", lambda r: WZ.at[7, 0, 0], lambda r: WZ.at[7, 0, NY - r], (2, 1, 3), WZ.at[7, 0, pl.ds(1, 3)])

    def z_across():
        zs["back_y"].arrive()
        zs["back_x"] = spread(
            "x", lambda r: WZ.at[7, 0], lambda r: WZ.at[7, NX - r], (2, 1, 3), WZ.at[7, pl.ds(1, 3)])

    def z_gather(step):
        if step == 0:
            zs["back_x"].arrive()
        else:
            zs["gather", step - 1].arrive()
        devs = both_ways("z")
        items = []
        for way in range(2):
            r = (NZ - step) % NZ if way == 0 else step
            land = NZ - step - 1 if way == 0 else step + 1
            for half in ((0, 1) if step < 3 else (way,)):
                rows = pl.ds(2 * half, 2)
                items.append((WZ.at[PLACE[r], rows], WZ.at[PLACE[land], rows], devs[way]))
        zs["gather", step] = Group(items, WZ.at[pl.ds(0, 2)] if step < 3 else WZ.at[0])

    def states():
        wait_bytes(MFS, bulk_sem.at[3])

    def rows_1():
        zs["g1"] = spread(
            "x", lambda r: GB.at[0, 0, 0], lambda r: GB.at[0, 0, NX - r], (2, 1, 3), GB.at[0, 0, pl.ds(1, 3)])

    def rows_2():
        zs["g1"].arrive()
        zs["g2"] = Group([(GB.at[0, 0], GB.at[0, 1], ahead["y", 2])], GB.at[0, 0])

    def rows_3():
        zs["g2"].arrive()
        zs["g3"] = Group([(GB.at[0], GB.at[1], mate)], GB.at[0])

    def moments(cr):
        def body(i, carry):
            yr, xr = i // 4, lax.rem(i, 4)
            side = core if cr == 0 else 1 - core
            row = side * 256 + lax.rem(x + xr, NX) * 64 + lax.rem(y_hi + yr, 2) * 32
            rows = pl.ds(pl.multiple_of(row, 32), 32)
            new_master, new_first, new_second = adam(
                GB[cr, yr, xr].astype(F32), *(MFS[j, rows, :] for j in range(3)))
            o_master[rows, :] = new_master
            o_first[rows, :] = new_first
            o_second[rows, :] = new_second
            return carry
        lax.fori_loop(0, 8, body, 0)

    def values(part):
        blocks = NZ // PARTS
        first = part * blocks
        for st in streams.values():
            for q in sorted({(first + i) // K for i in range(blocks)}):
                st.finish(q)
        for step in range(max(min(r, NZ - r) for r in ORDER[first:first + blocks])):
            zs["gather", step].arrive()

        def body(j, carry):
            y_lo = lax.rem(j, 2)
            k = first + j // 2
            q, kk = k // K, lax.rem(k, K)
            for g, xr, yr in groups(y_lo):
                def put(unit, w):
                    row, col = unit
                    at = pl.ds(pl.multiple_of(j * 256 + g * 32 + row * 16, 16), 16)
                    WT[at, col * 128:col * 128 + 128] = w
                for st in streams.values():
                    for i, unit in enumerate(st.units):
                        put(unit, st.W[st.places(xr, q, yr, kk, i)])
                for i, unit in enumerate(Z_UNITS):
                    put(unit, WZ[k, xr, yr, i])
            return carry
        lax.fori_loop(0, 2 * blocks, body, 0)
        product = jnp.dot(NB[part], WT[...], preferred_element_type=F32)
        if part == PARTS - 1:
            VO[...] = product
        else:
            VO[...] += product

    def nexts():
        wait_bytes(NB, bulk_sem.at[2])

    v_sem = arrival()

    def last_swap():
        VS[...] = VO[pl.ds(128, 128), :]
        Group([(VS, VR, mate)], VR, v_sem)
        wait_bytes(VR, v_sem)
        o_values[...] = (VO[pl.ds(0, 128), :] + VR[...]).astype(BF16)

    wait_bytes(CB, c_sem)
    gemm(0, 1)
    z_long(0)
    gemm(1, 2)
    x_s.hop0(0)
    y_s.hop0(0)
    gemm(2, 3)
    z_short(0)
    gemm(3, 4)
    states()
    x_s.hop0(1)
    y_s.hop0(1)
    gemm(4, 5)
    z_long(1)
    x_s.hop1(0)
    y_s.hop1(0)
    gemm(5, 6)
    y_s.hop0(2)
    x_s.hop0(2)
    z_short(1)
    x_s.hop1(1)
    gemm(6, 7)
    y_s.hop1(1)
    z_long(2)
    gemm(7, 8)
    x_s.hop0(3)
    x_s.second(0)
    y_s.hop0(3)
    z_short(2)
    x_s.hop1(2)
    z_long(3)
    y_s.hop1(2)
    y_s.second(1)
    x_s.hop1(3)
    x_s.second(1)
    x_s.third(0)
    y_s.second(0)
    y_s.hop1(3)
    nexts()
    x_s.second(2)
    z_second()
    y_s.third(1)
    y_s.second(2)
    x_s.second(3)
    x_s.third(1)
    y_s.second(3)
    y_s.third(0)
    x_s.third(2)
    z_third()
    x_s.third(3)
    y_s.third(2)
    y_s.third(3)
    z_update()
    x_s.update()
    y_s.update()
    rows_1()
    x_s.across(3)
    z_across()
    x_s.across(2)
    y_s.across(3)
    rows_2()
    x_s.across(1)
    y_s.across(2)
    x_s.go0(3)
    x_s.across(0)
    z_gather(0)
    y_s.across(1)
    y_s.go0(3)
    y_s.across(0)
    x_s.go0(2)
    y_s.go0(2)
    z_gather(1)
    y_s.go0(1)
    rows_3()
    x_s.go0(1)
    x_s.go1(3)
    x_s.go1(2)
    x_s.go0(0)
    y_s.go1(3)
    y_s.go0(0)
    z_gather(2)
    moments(0)
    x_s.go1(1)
    y_s.go1(2)
    y_s.go1(1)
    zs["g3"].arrive()
    moments(1)
    values(3)
    y_s.go1(0)
    z_gather(3)
    x_s.go1(0)
    values(2)
    values(1)
    values(0)
    last_swap()
    for group in pool:
        if group is not None:
            group.leave()
    wait_bytes(XB.at[pl.ds(0, 8)], bulk_sem.at[0])
    wait_bytes(NB.at[pl.ds(0, 2)], bulk_sem.at[1])


def place(a, b, c, d, o_a, o_b, o_c, o_d, sem):
    copies = [
        pltpu.make_async_copy(src, dst, sem.at[i])
        for i, (src, dst) in enumerate(((a, o_a), (b, o_b), (c, o_c), (d, o_d)))
    ]
    for copy in copies:
        copy.start()
    for copy in copies:
        copy.wait()


OUTS = (((512, 512), F32), ((512, 512), F32), ((512, 512), F32), ((128, 512), BF16))


def local_step(layer_input, value_cotangent, master_weight, first_moment, second_moment, next_input):
    unit = (16, 128)

    def vm(*shape, dtype=BF16):
        return pltpu.VMEM(shape, dtype)

    def stream_buffers(n):
        u = (n,) + unit
        return (
            vm(4, Q, 4, K, *u), vm(Q, 2, 2, K, *u), vm(Q, 4, 2, K, *u), vm(Q, 4, K, *u), vm(Q, 3, K, *u),
            vm(8, *u), vm(7, *u), vm(4, Q, 4, K, *u))

    half_z = (2, 4, 2) + unit
    scratch = [
        vm(16, 1024, 256), vm(1024, 512), vm(4, 256, 1024),
        vm(8, 4, 4, 2, *unit), vm(4, 2, *half_z), vm(3, 2, *half_z),
        vm(4, 4, 2, *unit), vm(3, 4, 2, *unit), vm(4, 2, *unit), vm(3, 2, *unit), vm(8, 4, 4, 2, *unit),
        *[stream_buffers(len(STREAMS[name][2])) for name in STREAMS],
        vm(2, 2, 4, 32, 512),
        vm(3, 512, 512, dtype=F32),
        vm(1024, 512), vm(256, 512, dtype=F32), vm(128, 512, dtype=F32), vm(128, 512, dtype=F32),
        pltpu.SemaphoreType.DMA((POOL,)), pltpu.SemaphoreType.DMA((ARRIVALS,)),
        pltpu.SemaphoreType.DMA((16,)), pltpu.SemaphoreType.DMA((4,)),
    ]
    results = pl.pallas_call(
        kernel,
        out_shape=tuple(pltpu.VMEM(shape, dtype) for shape, dtype in OUTS),
        in_specs=[pl.BlockSpec(memory_space=pl.ANY)] * 6,
        out_specs=(pl.BlockSpec(memory_space=pltpu.VMEM),) * 4,
        scratch_shapes=scratch,
        compiler_params=pltpu.CompilerParams(
            collective_id=0, has_side_effects=True, vmem_limit_bytes=56 * 2**20),
        cost_estimate=pl.CostEstimate(flops=5_400_000_000, bytes_accessed=18_000_000, transcendentals=0),
        name="value_projection_step",
    )(layer_input, value_cotangent, master_weight, first_moment, second_moment, next_input)
    return tuple(pl.pallas_call(
        place,
        out_shape=tuple(jax.ShapeDtypeStruct(shape, dtype) for shape, dtype in OUTS),
        in_specs=[pl.BlockSpec(memory_space=pltpu.VMEM)] * 4,
        out_specs=(pl.BlockSpec(memory_space=pl.ANY),) * 4,
        scratch_shapes=[pltpu.SemaphoreType.DMA((4,))],
        compiler_params=pltpu.CompilerParams(vmem_limit_bytes=2**20),
        name="place_results",
    )(*results))


def solution(mesh):
    in_specs = (
        P(("cuts", "fsdp"), None),
        P(("cuts", "fsdp"), None),
        P("fsdp", None),
        P("fsdp", None),
        P("fsdp", None),
        P(("cuts", "fsdp"), None),
    )
    out_specs = (P("fsdp", None), P("fsdp", None), P("fsdp", None), P(("cuts", "fsdp"), None))
    return jax.shard_map(local_step, mesh=mesh, in_specs=in_specs, out_specs=out_specs, check_vma=False)
```

```python
import functools

import jax
import jax.numpy as jnp
from jax import lax
from jax.experimental import pallas as pl
from jax.experimental.pallas import tpu as pltpu
from jax.sharding import PartitionSpec as P

STEP = 200
beta_first = 0.9
beta_second = 0.95
learn_rate = 0.001
epsilon = 1e-08

MESH = pl.DeviceIdType.MESH
BF16 = jnp.bfloat16
F32 = jnp.float32

NX, NY, NZ = 4, 4, 8
POOL = 24
ARRIVALS = 80
AXES = {"x": NX, "y": NY, "z": NZ}
ORDER = (4, 3, 5, 2, 6, 1, 7, 0)
PLACE = {r: k for k, r in enumerate(ORDER)}
GROUPS = (1, 2, 2, 3)
START = tuple(sum(GROUPS[:q]) for q in range(len(GROUPS)))
GROUP = tuple(q for q, size in enumerate(GROUPS) for _ in range(size))
Q = len(GROUPS)
STREAMS = {
    "x": ("x", "y", [(0, 0), (0, 1), (0, 2)]),
    "y": ("y", "x", [(0, 3), (1, 0), (1, 1)]),
}
Z_UNITS = [(1, 2), (1, 3)]


def position():
    cuts, fsdp = lax.axis_index("cuts"), lax.axis_index("fsdp")
    x, y_hi, core = cuts // 4, lax.rem(cuts // 2, 2), lax.rem(cuts, 2)
    z, y_lo = fsdp // 2, lax.rem(fsdp, 2)
    return x, y_hi * 2 + y_lo, z, core


def device(x, y, z, core):
    return (x * 4 + (y // 2) * 2 + core, z * 2 + lax.rem(y, 2))


def kernel(
    x_hbm, c_hbm, master_hbm, first_hbm, second_hbm, next_hbm,
    o_master, o_first, o_second, o_values,
    XB, CB, NB, PZ, RZL, RZS, S2Z, R2Z, S3Z, R3Z, WZ,
    buf_x, buf_y,
    GB, MFS, WT, VO, VR,
    send_sem, recv_sem, x_sem, bulk_sem,
):
    x, y, z, core = position()
    here = {"x": x, "y": y, "z": z}

    def towards(axis, delta):
        at = dict(here)
        at[axis] = lax.rem(here[axis] + delta, AXES[axis])
        return device(at["x"], at["y"], at["z"], core)

    mate = device(x, y, z, 1 - core)
    ahead = {(a, d): towards(a, d) for a in "xyz" for d in range(1, AXES[a])}

    barrier = pltpu.get_barrier_semaphore()
    partners = [mate] + [ahead[key] for key in sorted(ahead, key=lambda p: -min(p[1], AXES[p[0]] - p[1]))]
    for dev in partners:
        pl.semaphore_signal(barrier, inc=1, device_id=dev, device_id_type=MESH)

    counts = {"arrival": 0, "group": 0}
    pool = [None] * POOL

    def arrival():
        counts["arrival"] += 1
        return recv_sem.at[counts["arrival"] - 1]

    def wait_bytes(ref, sem):
        pltpu.make_async_copy(ref, ref, sem).wait()

    class Group:
        def __init__(self, items, whole, recv=None):
            slot = counts["group"] % POOL
            counts["group"] += 1
            if pool[slot] is not None:
                pool[slot].leave()
            pool[slot] = self
            self.whole, self.sem = whole, send_sem.at[slot]
            self.recv = arrival() if recv is None else None
            self.landed = recv is not None
            for i, (src, dst, dev) in enumerate(items):
                sem = self.recv if recv is None else recv[i] if isinstance(recv, list) else recv
                pltpu.make_async_remote_copy(
                    src_ref=src, dst_ref=dst, send_sem=self.sem, recv_sem=sem,
                    device_id=dev, device_id_type=MESH,
                ).start()

        def leave(self):
            wait_bytes(self.whole, self.sem)

        def arrive(self):
            if not self.landed:
                self.landed = True
                wait_bytes(self.whole, self.recv)

    def block_of(t):
        k = t // 2
        odd = lax.rem(k, 2)
        r = 4 + (1 - odd) * (k // 2) - odd * ((k + 1) // 2)
        return lax.rem(z + r, NZ) * 2 + lax.rem(t, 2)

    def columns(t, side):
        return pl.ds(pl.multiple_of(block_of(t) * 512 + side * 256, 256), 256)

    def x_load(t):
        return pltpu.make_async_copy(
            x_hbm.at[:, columns(t, core)], XB.at[t, pl.ds(0, 512)], x_sem.at[t])

    def x_push(t):
        return pltpu.make_async_remote_copy(
            src_ref=x_hbm.at[:, columns(t, 1 - core)], dst_ref=XB.at[t, pl.ds(512, 512)],
            send_sem=bulk_sem.at[0], recv_sem=x_sem.at[t], device_id=mate, device_id_type=MESH)

    def n_place(t, rows):
        return NB.at[pl.ds(rows, 128), pl.ds(pl.multiple_of(t * 256, 256), 256)]

    def n_load(t):
        return pltpu.make_async_copy(next_hbm.at[:, columns(t, core)], n_place(t, 0), bulk_sem.at[2])

    def n_push(t):
        return pltpu.make_async_remote_copy(
            src_ref=next_hbm.at[:, columns(t, 1 - core)], dst_ref=n_place(t, 128),
            send_sem=bulk_sem.at[1], recv_sem=bulk_sem.at[2], device_id=mate, device_id_type=MESH)

    def each(n, act):
        def body(t, carry):
            act(t)
            return carry
        lax.fori_loop(0, n, body, 0)

    c_sem = arrival()
    pltpu.make_async_copy(c_hbm, CB.at[pl.ds(0, 512)], c_sem).start()
    each(16, lambda t: x_load(t).start())
    pl.semaphore_wait(barrier, len(partners))

    Group([(c_hbm, CB.at[pl.ds(512, 512)], mate)], CB.at[pl.ds(512, 512)], c_sem)
    each(16, lambda t: x_push(t).start())
    for i, ref in enumerate((master_hbm, first_hbm, second_hbm)):
        pltpu.make_async_copy(ref, MFS.at[i], bulk_sem.at[3]).start()
    each(16, lambda t: n_load(t).start())
    each(16, lambda t: n_push(t).start())

    def groups(y_lo):
        out = []
        for g in range(8):
            xr = lax.rem(g // 2 + NX - x, NX)
            yr = lax.rem((g % 2) * 2 + y_lo + NY - y, NY)
            out.append((g, xr, yr))
        return out

    def tile(k, y_lo, carry):
        t = 2 * k + y_lo
        wait_bytes(XB.at[t], x_sem.at[t])
        g_tile = lax.dot_general(
            XB[t], CB[...], (((0,), (0,)), ((), ())), preferred_element_type=F32).astype(BF16)
        q, kk = GROUP[k], k - START[GROUP[k]]

        def piece(g, unit):
            row, col = unit
            return g_tile[g * 32 + row * 16:g * 32 + row * 16 + 16, col * 128:col * 128 + 128]

        for g, xr, yr in groups(y_lo):
            for st in streams.values():
                for i, unit in enumerate(st.units):
                    st.P[q][st.places(xr, yr, kk, i)] = piece(g, unit)
            for i, unit in enumerate(Z_UNITS):
                PZ[k, xr, yr, i] = piece(g, unit)
        return carry

    def gemm(first, last):
        for k in range(first, last):
            lax.fori_loop(0, 2, functools.partial(tile, k), 0)

    def add_rows(dst, terms, n):
        def body(i, carry):
            total = terms[0][i].astype(F32)
            for term in terms[1:]:
                total = total + term[i].astype(F32)
            dst[i] = total.astype(dst.dtype)
            return carry
        lax.fori_loop(0, n, body, 0)

    def both_ways(axis):
        return ahead[axis, 1], ahead[axis, AXES[axis] - 1]

    class Ring:
        def __init__(self, axis, chunk, long_buf, short_buf, rows):
            self.axis, self.chunk, self.long_buf, self.short_buf, self.rows = axis, chunk, long_buf, short_buf, rows
            self.n = AXES[axis]
            self.long, self.short, self.last = {}, {}, None

        def _send(self, copies, buf, step, dist, halves, recv=None):
            chunks = [self.chunk(dist, halves[0]), self.chunk(self.n - dist, halves[1])]
            if step > 0:
                copies[step - 1].arrive()
                for way in range(2):
                    add_rows(chunks[way], [chunks[way], buf.at[step - 1, way]], self.rows)
            devs = both_ways(self.axis)
            copies[step] = Group([(chunks[w], buf.at[step, w], devs[w]) for w in range(2)], buf.at[step], recv)

        def send_long(self, step, recv=None):
            self._send(self.long, self.long_buf, step, self.n // 2 - step, (0, 1), recv)

        def send_short(self, step, recv=None):
            self._send(self.short, self.short_buf, step, self.n // 2 - 1 - step, (1, 0), recv)

        def total(self, dst):
            n = self.n
            for half in range(2):
                add_rows(dst(half), [
                    self.chunk(0, half),
                    self.long_buf.at[n // 2 - 1, half],
                    self.short_buf.at[n // 2 - 2, 1 - half],
                ], self.rows)

    def spread(axis, src, dst, order, whole, recv=None):
        return Group([(src(r), dst(r), ahead[axis, r]) for r in order], whole, recv)

    ring_z = Ring("z", lambda r, h: PZ.at[PLACE[r], pl.ds(2 * h, 2)], RZL, RZS, 2)

    def z_long(step):
        ring_z.send_long(step)

    def z_short(step):
        ring_z.send_short(step)

    def adam(gradient, master, first, second):
        new_first = beta_first * first + (1.0 - beta_first) * gradient
        new_second = beta_second * second + (1.0 - beta_second) * gradient * gradient
        first_hat = new_first / (1.0 - beta_first**STEP)
        second_hat = new_second / (1.0 - beta_second**STEP)
        new_master = master - learn_rate * first_hat / (jnp.sqrt(second_hat) + epsilon)
        return new_master, new_first, new_second

    y_hi = y // 2
    own_row = core * 256 + x * 64 + y_hi * 32

    def own_update(units, own, received, n, dst):
        for n_unit, (row, col) in enumerate(units):
            gradient = own[n_unit].astype(F32)
            for s in range(n):
                gradient = gradient + received[s, n_unit].astype(F32)
            gradient = gradient.astype(BF16)
            GB[0, 0, 0, row * 16:row * 16 + 16, col * 128:col * 128 + 128] = gradient
            rows = pl.ds(pl.multiple_of(own_row + row * 16, 16), 16)
            cols = slice(col * 128, col * 128 + 128)
            new_master, _, _ = adam(gradient.astype(F32), *(MFS[i, rows, cols] for i in range(3)))
            dst[n_unit] = new_master.astype(BF16)

    near_first = (1, 7, 2, 6, 3, 5, 4)

    class Stream:
        def __init__(self, name, bufs):
            self.axis, self.other, self.units = STREAMS[name]
            self.P, self.RL, self.RS, self.S2, self.R2, self.S3, self.R3, self.W = bufs
            self.two, self.near, self.across_, self.long = {}, {}, {}, {}
            self.ring_last = [arrival() for _ in range(Q)]
            self.gather_last = [arrival() for _ in range(Q)]
            self.back = [arrival() for _ in range(Q)]
            self.three = arrival()
            self.done = set()

        def half(self, r, q, h):
            return self.P[q].at[r, pl.ds(2 * h, 2)]

        def part(self, r, q, h):
            return self.W[q].at[r, pl.ds(2 * h, 2)]

        def places(self, xr, yr, kk, i):
            return (xr, yr, kk, i) if self.axis == "x" else (yr, xr, kk, i)

        def hop0(self, q):
            devs = both_ways(self.axis)
            self.near[q] = Group(
                [(self.half(2, q, w), self.RL[q].at[w], devs[w]) for w in range(2)], self.RL[q])
            Group(
                [(self.half(1 + 2 * w, q, 1 - w), self.RS[q].at[2 + w], devs[w]) for w in range(2)],
                self.RL[q], self.ring_last[q])

        def hop1(self, q):
            devs = both_ways(self.axis)
            self.near[q].arrive()
            for w in range(2):
                chunk = self.half(1 + 2 * w, q, w)
                add_rows(chunk, [chunk, self.RL[q].at[w]], 2)
            Group(
                [(self.half(1 + 2 * w, q, w), self.RS[q].at[w], devs[w]) for w in range(2)],
                self.RL[q], self.ring_last[q])

        def second(self, q):
            wait_bytes(self.RS[q], self.ring_last[q])
            for h in range(2):
                add_rows(
                    self.S2[q].at[pl.ds(2 * h, 2)], [self.half(0, q, h), self.RS[q].at[h], self.RS[q].at[3 - h]], 2)
            self.two[q] = spread(
                self.other, lambda r: self.S2[q].at[r], lambda r: self.R2[q].at[r - 1], (2, 1, 3), self.R2[q])

        def third(self, q):
            self.two[q].arrive()
            add_rows(self.S3.at[pl.ds(START[q], GROUPS[q])], [self.S2[q].at[0]] + [self.R2[q].at[r] for r in range(3)], GROUPS[q])
            order = [r for r in ORDER[START[q]:START[q] + GROUPS[q]] if r > 0]
            spread("z", lambda r: self.S3.at[PLACE[r]], lambda r: self.R3.at[r - 1], order,
                   self.S3.at[pl.ds(START[q], len(order))], self.three)

        def own(self, r):
            return self.W[GROUP[PLACE[r]]].at[0, 0, PLACE[r] - START[GROUP[PLACE[r]]]]

        def update(self):
            wait_bytes(self.R3, self.three)
            own_update(self.units, self.S3.at[7], self.R3, 7, self.own(0))
            spread("z", lambda r: self.own(0), lambda r: self.own(NZ - r), near_first, self.R3,
                   [self.back[GROUP[PLACE[NZ - r]]] for r in near_first])

        def across(self, q):
            came = len([r for r in ORDER[START[q]:START[q] + GROUPS[q]] if r > 0])
            wait_bytes(self.W[q].at[0, 0, pl.ds(0, came)], self.back[q])
            self.across_[q] = spread(
                self.other, lambda r: self.W[q].at[0, 0], lambda r: self.W[q].at[0, 4 - r], (2, 1, 3),
                self.W[q].at[0, pl.ds(1, 3)])

        def go0(self, q):
            devs = both_ways(self.axis)
            self.across_[q].arrive()
            self.long[q] = Group(
                [(self.part(0, q, w), self.part(3 - 2 * w, q, w), devs[w]) for w in range(2)], self.W[q].at[0])
            Group(
                [(self.part(0, q, 1 - w), self.part(3 - 2 * w, q, 1 - w), devs[w]) for w in range(2)],
                self.W[q].at[0], self.gather_last[q])

        def go1(self, q):
            devs = both_ways(self.axis)
            self.long[q].arrive()
            Group(
                [(self.part(3 - 2 * w, q, w), self.part(2, q, w), devs[w]) for w in range(2)],
                self.W[q].at[0], self.gather_last[q])

        def finish(self, q):
            if q not in self.done:
                self.done.add(q)
                wait_bytes(self.W[q].at[pl.ds(0, 2)], self.gather_last[q])

    streams = {name: Stream(name, bufs) for name, bufs in zip(STREAMS, (buf_x, buf_y))}
    x_s, y_s = streams.values()
    zs = {}

    def z_second():
        ring_z.long[3].arrive()
        ring_z.short[2].arrive()
        ring_z.total(lambda half: S2Z.at[pl.ds(2 * half, 2)])
        zs["two"] = spread("x", lambda r: S2Z.at[r], lambda r: R2Z.at[r - 1], (2, 1, 3), R2Z)

    def z_third():
        zs["two"].arrive()
        add_rows(S3Z, [S2Z.at[0], R2Z.at[0], R2Z.at[1], R2Z.at[2]], 4)
        zs["three"] = spread("y", lambda r: S3Z.at[r], lambda r: R3Z.at[r - 1], (2, 1, 3), R3Z)

    def z_update():
        zs["three"].arrive()
        own_update(Z_UNITS, S3Z.at[0], R3Z, 3, WZ.at[7, 0, 0])
        zs["back_y"] = spread(
            "y", lambda r: WZ.at[7, 0, 0], lambda r: WZ.at[7, 0, NY - r], (2, 1, 3), WZ.at[7, 0, pl.ds(1, 3)])

    def z_across():
        zs["back_y"].arrive()
        zs["back_x"] = spread(
            "x", lambda r: WZ.at[7, 0], lambda r: WZ.at[7, NX - r], (2, 1, 3), WZ.at[7, pl.ds(1, 3)])

    def z_gather(step):
        if step == 0:
            zs["back_x"].arrive()
        else:
            zs["gather", step - 1].arrive()
        devs = both_ways("z")
        items = []
        for way in range(2):
            r = (NZ - step) % NZ if way == 0 else step
            land = NZ - step - 1 if way == 0 else step + 1
            for half in ((0, 1) if step < 3 else (way,)):
                rows = pl.ds(2 * half, 2)
                items.append((WZ.at[PLACE[r], rows], WZ.at[PLACE[land], rows], devs[way]))
        zs["gather", step] = Group(items, WZ.at[pl.ds(0, 2)] if step < 3 else WZ.at[0])

    def states():
        wait_bytes(MFS, bulk_sem.at[3])

    def rows_1():
        zs["g1"] = spread(
            "x", lambda r: GB.at[0, 0, 0], lambda r: GB.at[0, 0, NX - r], (2, 1, 3), GB.at[0, 0, pl.ds(1, 3)])

    def rows_2():
        zs["g1"].arrive()
        zs["g2"] = Group([(GB.at[0, 0], GB.at[0, 1], ahead["y", 2])], GB.at[0, 0])

    def rows_3():
        zs["g2"].arrive()
        zs["g3"] = Group([(GB.at[0], GB.at[1], mate)], GB.at[0])

    def moments(cr):
        def body(i, carry):
            yr, xr = i // 4, lax.rem(i, 4)
            side = core if cr == 0 else 1 - core
            row = side * 256 + lax.rem(x + xr, NX) * 64 + lax.rem(y_hi + yr, 2) * 32
            rows = pl.ds(pl.multiple_of(row, 32), 32)
            new_master, new_first, new_second = adam(
                GB[cr, yr, xr].astype(F32), *(MFS[j, rows, :] for j in range(3)))
            o_master[rows, :] = new_master
            o_first[rows, :] = new_first
            o_second[rows, :] = new_second
            return carry
        lax.fori_loop(0, 8, body, 0)

    v_sem = arrival()

    def values(part):
        blocks, first = GROUPS[part], START[part]
        for st in streams.values():
            st.finish(part)
        for step in range(max(min(r, NZ - r) for r in ORDER[first:first + blocks])):
            zs["gather", step].arrive()

        def body(j, carry):
            y_lo = lax.rem(j, 2)
            k = first + j // 2
            for g, xr, yr in groups(y_lo):
                def put(unit, w):
                    row, col = unit
                    at = pl.ds(pl.multiple_of(j * 256 + g * 32 + row * 16, 16), 16)
                    WT[at, col * 128:col * 128 + 128] = w
                for st in streams.values():
                    for i, unit in enumerate(st.units):
                        put(unit, st.W[part][st.places(xr, yr, j // 2, i)])
                for i, unit in enumerate(Z_UNITS):
                    put(unit, WZ[k, xr, yr, i])
            return carry
        lax.fori_loop(0, 2 * blocks, body, 0)
        cols, rows = pl.ds(first * 512, blocks * 512), pl.ds(0, blocks * 512)
        if part == Q - 1:
            VO[...] = jnp.dot(NB[:, cols], WT[rows, :], preferred_element_type=F32)
        elif part > 0:
            VO[...] += jnp.dot(NB[:, cols], WT[rows, :], preferred_element_type=F32)
        else:
            theirs, ours = pl.ds(128, 128), pl.ds(0, 128)
            VO[theirs, :] += jnp.dot(NB[theirs, cols], WT[rows, :], preferred_element_type=F32)
            Group([(VO.at[theirs], VR, mate)], VR, v_sem)
            VO[ours, :] += jnp.dot(NB[ours, cols], WT[rows, :], preferred_element_type=F32)

    def nexts():
        wait_bytes(NB, bulk_sem.at[2])

    def last_swap():
        wait_bytes(VR, v_sem)
        o_values[...] = (VO[pl.ds(0, 128), :] + VR[...]).astype(BF16)

    wait_bytes(CB, c_sem)
    gemm(0, 1)
    z_long(0)
    y_s.hop0(0)
    x_s.hop0(0)
    gemm(1, 3)
    x_s.hop0(1)
    y_s.hop0(1)
    z_short(0)
    gemm(3, 5)
    y_s.hop1(0)
    y_s.hop0(2)
    x_s.hop1(0)
    x_s.hop0(2)
    z_long(1)
    gemm(5, 8)
    x_s.hop1(1)
    states()
    z_short(1)
    y_s.hop1(1)
    x_s.hop0(3)
    y_s.second(0)
    y_s.hop0(3)
    x_s.second(0)
    x_s.hop1(2)
    z_long(2)
    y_s.hop1(2)
    z_short(2)
    x_s.hop1(3)
    z_long(3)
    x_s.second(1)
    y_s.second(1)
    y_s.hop1(3)
    y_s.second(2)
    y_s.third(0)
    x_s.third(0)
    x_s.second(2)
    z_second()
    x_s.second(3)
    y_s.second(3)
    x_s.third(1)
    x_s.third(2)
    y_s.third(1)
    z_third()
    x_s.third(3)
    y_s.third(2)
    y_s.third(3)
    x_s.update()
    z_update()
    nexts()
    y_s.update()
    rows_1()
    x_s.across(3)
    z_across()
    x_s.across(2)
    y_s.across(3)
    rows_2()
    y_s.across(2)
    x_s.across(1)
    z_gather(0)
    y_s.across(1)
    x_s.go0(3)
    x_s.across(0)
    y_s.go0(3)
    y_s.across(0)
    y_s.go0(2)
    x_s.go0(1)
    z_gather(1)
    y_s.go0(1)
    rows_3()
    moments(0)
    x_s.go0(2)
    y_s.go1(3)
    zs["g3"].arrive()
    moments(1)
    y_s.go0(0)
    x_s.go0(0)
    y_s.go1(2)
    x_s.go1(3)
    z_gather(2)
    x_s.go1(2)
    y_s.go1(1)
    x_s.go1(1)
    z_gather(3)
    x_s.go1(0)
    y_s.go1(0)
    values(3)
    values(2)
    values(1)
    values(0)
    last_swap()
    for group in pool:
        if group is not None:
            group.leave()
    wait_bytes(XB.at[pl.ds(0, 8)], bulk_sem.at[0])
    wait_bytes(NB.at[pl.ds(0, 128)], bulk_sem.at[1])


def place(a, b, c, d, o_a, o_b, o_c, o_d, sem):
    copies = [
        pltpu.make_async_copy(src, dst, sem.at[i])
        for i, (src, dst) in enumerate(((a, o_a), (b, o_b), (c, o_c), (d, o_d)))
    ]
    for copy in copies:
        copy.start()
    for copy in copies:
        copy.wait()


OUTS = (((512, 512), F32), ((512, 512), F32), ((512, 512), F32), ((128, 512), BF16))


def local_step(layer_input, value_cotangent, master_weight, first_moment, second_moment, next_input):
    unit = (16, 128)

    def vm(*shape, dtype=BF16):
        return pltpu.VMEM(shape, dtype)

    def stream_buffers(n):
        u = (n,) + unit
        def each(*dims):
            return tuple(vm(*dims, size, *u) for size in GROUPS)

        return (each(4, 4), each(2, 2), each(4, 2), each(4), each(3), vm(8, *u), vm(7, *u), each(4, 4))

    half_z = (2, 4, 2) + unit
    scratch = [
        vm(16, 1024, 256), vm(1024, 512), vm(256, 4096),
        vm(8, 4, 4, 2, *unit), vm(4, 2, *half_z), vm(3, 2, *half_z),
        vm(4, 4, 2, *unit), vm(3, 4, 2, *unit), vm(4, 2, *unit), vm(3, 2, *unit), vm(8, 4, 4, 2, *unit),
        *[stream_buffers(len(STREAMS[name][2])) for name in STREAMS],
        vm(2, 2, 4, 32, 512),
        vm(3, 512, 512, dtype=F32),
        vm(512 * max(GROUPS), 512), vm(256, 512, dtype=F32), vm(128, 512, dtype=F32),
        pltpu.SemaphoreType.DMA((POOL,)), pltpu.SemaphoreType.DMA((ARRIVALS,)),
        pltpu.SemaphoreType.DMA((16,)), pltpu.SemaphoreType.DMA((4,)),
    ]
    results = pl.pallas_call(
        kernel,
        out_shape=tuple(pltpu.VMEM(shape, dtype) for shape, dtype in OUTS),
        in_specs=[pl.BlockSpec(memory_space=pl.ANY)] * 6,
        out_specs=(pl.BlockSpec(memory_space=pltpu.VMEM),) * 4,
        scratch_shapes=scratch,
        compiler_params=pltpu.CompilerParams(
            collective_id=0, has_side_effects=True, vmem_limit_bytes=56 * 2**20),
        cost_estimate=pl.CostEstimate(flops=5_400_000_000, bytes_accessed=18_000_000, transcendentals=0),
        name="value_projection_step",
    )(layer_input, value_cotangent, master_weight, first_moment, second_moment, next_input)
    return tuple(pl.pallas_call(
        place,
        out_shape=tuple(jax.ShapeDtypeStruct(shape, dtype) for shape, dtype in OUTS),
        in_specs=[pl.BlockSpec(memory_space=pltpu.VMEM)] * 4,
        out_specs=(pl.BlockSpec(memory_space=pl.ANY),) * 4,
        scratch_shapes=[pltpu.SemaphoreType.DMA((4,))],
        compiler_params=pltpu.CompilerParams(vmem_limit_bytes=2**20),
        name="place_results",
    )(*results))


def solution(mesh):
    in_specs = (
        P(("cuts", "fsdp"), None),
        P(("cuts", "fsdp"), None),
        P("fsdp", None),
        P("fsdp", None),
        P("fsdp", None),
        P(("cuts", "fsdp"), None),
    )
    out_specs = (P("fsdp", None), P("fsdp", None), P("fsdp", None), P(("cuts", "fsdp"), None))
    return jax.shard_map(local_step, mesh=mesh, in_specs=in_specs, out_specs=out_specs, check_vma=False)
```

```python
import functools

import jax
import jax.numpy as jnp
from jax import lax
from jax.experimental import pallas as pl
from jax.experimental.pallas import tpu as pltpu
from jax.sharding import PartitionSpec as P

STEP = 200
beta_first = 0.9
beta_second = 0.95
learn_rate = 0.001
epsilon = 1e-08

MESH = pl.DeviceIdType.MESH
BF16 = jnp.bfloat16
F32 = jnp.float32

NX, NY, NZ = 4, 4, 8
POOL = 12
ARRIVALS = 70
AXES = {"x": NX, "y": NY, "z": NZ}
ORDER = (4, 3, 5, 2, 6, 1, 7, 0)
PLACE = {r: k for k, r in enumerate(ORDER)}
GROUPS = (1, 2, 2, 3)
START = tuple(sum(GROUPS[:q]) for q in range(len(GROUPS)))
GROUP = tuple(q for q, size in enumerate(GROUPS) for _ in range(size))
Q = len(GROUPS)
STREAMS = {
    "x": ("x", "y", [(0, 0), (0, 1), (0, 2)]),
    "y": ("y", "x", [(0, 3), (1, 0), (1, 1)]),
}
Z_UNITS = [(1, 2), (1, 3)]


def position():
    cuts, fsdp = lax.axis_index("cuts"), lax.axis_index("fsdp")
    x, y_hi, core = cuts // 4, lax.rem(cuts // 2, 2), lax.rem(cuts, 2)
    z, y_lo = fsdp // 2, lax.rem(fsdp, 2)
    return x, y_hi * 2 + y_lo, z, core


def device(x, y, z, core):
    return (x * 4 + (y // 2) * 2 + core, z * 2 + lax.rem(y, 2))


def kernel(
    x_hbm, c_hbm, master_hbm, first_hbm, second_hbm, next_hbm,
    o_master, o_first, o_second, o_values,
    XB, CB, NB, PZ, RZL, RZS, S2Z, R2Z, S3Z, R3Z, WZ,
    buf_x, buf_y,
    GB, MFS, WT, VO, VR,
    send_sem, recv_sem, x_sem, bulk_sem,
):
    x, y, z, core = position()
    here = {"x": x, "y": y, "z": z}

    def towards(axis, delta):
        at = dict(here)
        at[axis] = lax.rem(here[axis] + delta, AXES[axis])
        return device(at["x"], at["y"], at["z"], core)

    mate = device(x, y, z, 1 - core)
    ahead = {(a, d): towards(a, d) for a in "xyz" for d in range(1, AXES[a])}

    barrier = pltpu.get_barrier_semaphore()
    partners = [mate] + [ahead[key] for key in sorted(ahead, key=lambda p: -min(p[1], AXES[p[0]] - p[1]))]
    for dev in partners:
        pl.semaphore_signal(barrier, inc=1, device_id=dev, device_id_type=MESH)

    counts = {"arrival": 0, "group": 0}
    pool = [None] * POOL

    def arrival():
        counts["arrival"] += 1
        return recv_sem.at[counts["arrival"] - 1]

    def wait_bytes(ref, sem):
        pltpu.make_async_copy(ref, ref, sem).wait()

    class Group:
        def __init__(self, items, whole, recv=None):
            slot = counts["group"] % POOL
            counts["group"] += 1
            if pool[slot] is not None:
                pool[slot].leave()
            pool[slot] = self
            self.whole, self.sem = whole, send_sem.at[slot]
            self.recv = arrival() if recv is None else None
            self.landed = recv is not None
            for i, (src, dst, dev) in enumerate(items):
                sem = self.recv if recv is None else recv[i] if isinstance(recv, list) else recv
                pltpu.make_async_remote_copy(
                    src_ref=src, dst_ref=dst, send_sem=self.sem, recv_sem=sem,
                    device_id=dev, device_id_type=MESH,
                ).start()

        def leave(self):
            wait_bytes(self.whole, self.sem)

        def arrive(self):
            if not self.landed:
                self.landed = True
                wait_bytes(self.whole, self.recv)

    def block_of(t):
        k = t // 2
        odd = lax.rem(k, 2)
        r = 4 + (1 - odd) * (k // 2) - odd * ((k + 1) // 2)
        return lax.rem(z + r, NZ) * 2 + lax.rem(t, 2)

    def columns(t, side):
        return pl.ds(pl.multiple_of(block_of(t) * 512 + side * 256, 256), 256)

    def x_load(t):
        return pltpu.make_async_copy(
            x_hbm.at[:, columns(t, core)], XB.at[t, pl.ds(0, 512)], x_sem.at[t])

    def x_push(t):
        return pltpu.make_async_remote_copy(
            src_ref=x_hbm.at[:, columns(t, 1 - core)], dst_ref=XB.at[t, pl.ds(512, 512)],
            send_sem=bulk_sem.at[0], recv_sem=x_sem.at[t], device_id=mate, device_id_type=MESH)

    def n_place(t, rows):
        return NB.at[pl.ds(rows, 128), pl.ds(pl.multiple_of(t * 256, 256), 256)]

    def n_load(t):
        return pltpu.make_async_copy(next_hbm.at[:, columns(t, core)], n_place(t, 0), bulk_sem.at[2])

    def n_push(t):
        return pltpu.make_async_remote_copy(
            src_ref=next_hbm.at[:, columns(t, 1 - core)], dst_ref=n_place(t, 128),
            send_sem=bulk_sem.at[1], recv_sem=bulk_sem.at[2], device_id=mate, device_id_type=MESH)

    def each(n, act):
        def body(t, carry):
            act(t)
            return carry
        lax.fori_loop(0, n, body, 0)

    c_sem = arrival()
    pltpu.make_async_copy(c_hbm, CB.at[pl.ds(0, 512)], c_sem).start()
    each(2, lambda t: x_load(t).start())
    pl.semaphore_wait(barrier, len(partners))

    Group([(c_hbm, CB.at[pl.ds(512, 512)], mate)], CB.at[pl.ds(512, 512)], c_sem)
    each(4, lambda t: x_push(t).start())
    each(14, lambda t: x_load(t + 2).start())
    each(12, lambda t: x_push(t + 4).start())
    for i, ref in enumerate((master_hbm, first_hbm, second_hbm)):
        pltpu.make_async_copy(ref, MFS.at[i], bulk_sem.at[3]).start()
    each(16, lambda t: n_load(t).start())
    each(16, lambda t: n_push(t).start())

    def groups(y_lo):
        out = []
        for g in range(8):
            xr = lax.rem(g // 2 + NX - x, NX)
            yr = lax.rem((g % 2) * 2 + y_lo + NY - y, NY)
            out.append((g, xr, yr))
        return out

    def tile(k, y_lo, carry):
        t = 2 * k + y_lo
        wait_bytes(XB.at[t], x_sem.at[t])
        g_tile = lax.dot_general(
            XB[t], CB[...], (((0,), (0,)), ((), ())), preferred_element_type=F32).astype(BF16)
        q, kk = GROUP[k], k - START[GROUP[k]]

        def piece(g, unit):
            row, col = unit
            return g_tile[g * 32 + row * 16:g * 32 + row * 16 + 16, col * 128:col * 128 + 128]

        for g, xr, yr in groups(y_lo):
            for st in streams.values():
                for i, unit in enumerate(st.units):
                    st.P[q][st.places(xr, yr, kk, i)] = piece(g, unit)
            for i, unit in enumerate(Z_UNITS):
                PZ[k, xr, yr, i] = piece(g, unit)
        return carry

    def gemm(first, last):
        for k in range(first, last):
            lax.fori_loop(0, 2, functools.partial(tile, k), 0)

    def add_rows(dst, terms, n):
        def body(i, carry):
            total = terms[0][i].astype(F32)
            for term in terms[1:]:
                total = total + term[i].astype(F32)
            dst[i] = total.astype(dst.dtype)
            return carry
        lax.fori_loop(0, n, body, 0)

    def both_ways(axis):
        return ahead[axis, 1], ahead[axis, AXES[axis] - 1]

    class Ring:
        def __init__(self, axis, chunk, long_buf, short_buf, rows):
            self.axis, self.chunk, self.long_buf, self.short_buf, self.rows = axis, chunk, long_buf, short_buf, rows
            self.n = AXES[axis]
            self.long, self.short, self.last = {}, {}, None

        def _send(self, copies, buf, step, dist, halves, recv=None):
            chunks = [self.chunk(dist, halves[0]), self.chunk(self.n - dist, halves[1])]
            if step > 0:
                copies[step - 1].arrive()
                for way in range(2):
                    add_rows(chunks[way], [chunks[way], buf.at[step - 1, way]], self.rows)
            devs = both_ways(self.axis)
            copies[step] = Group([(chunks[w], buf.at[step, w], devs[w]) for w in range(2)], buf.at[step], recv)

        def send_long(self, step, recv=None):
            self._send(self.long, self.long_buf, step, self.n // 2 - step, (0, 1), recv)

        def send_short(self, step, recv=None):
            self._send(self.short, self.short_buf, step, self.n // 2 - 1 - step, (1, 0), recv)

        def total(self, dst):
            n = self.n
            for half in range(2):
                add_rows(dst(half), [
                    self.chunk(0, half),
                    self.long_buf.at[n // 2 - 1, half],
                    self.short_buf.at[n // 2 - 2, 1 - half],
                ], self.rows)

    def spread(axis, src, dst, order, whole, recv=None):
        return Group([(src(r), dst(r), ahead[axis, r]) for r in order], whole, recv)

    ring_z = Ring("z", lambda r, h: PZ.at[PLACE[r], pl.ds(2 * h, 2)], RZL, RZS, 2)

    def z_long(step):
        ring_z.send_long(step)

    def z_short(step):
        ring_z.send_short(step)

    def adam(gradient, master, first, second):
        new_first = beta_first * first + (1.0 - beta_first) * gradient
        new_second = beta_second * second + (1.0 - beta_second) * gradient * gradient
        first_hat = new_first / (1.0 - beta_first**STEP)
        second_hat = new_second / (1.0 - beta_second**STEP)
        new_master = master - learn_rate * first_hat / (jnp.sqrt(second_hat) + epsilon)
        return new_master, new_first, new_second

    y_hi = y // 2
    own_row = core * 256 + x * 64 + y_hi * 32

    def own_update(units, own, received, n, dst):
        for n_unit, (row, col) in enumerate(units):
            gradient = own[n_unit].astype(F32)
            for s in range(n):
                gradient = gradient + received[s, n_unit].astype(F32)
            gradient = gradient.astype(BF16)
            GB[0, 0, 0, row * 16:row * 16 + 16, col * 128:col * 128 + 128] = gradient
            rows = pl.ds(pl.multiple_of(own_row + row * 16, 16), 16)
            cols = slice(col * 128, col * 128 + 128)
            new_master, _, _ = adam(gradient.astype(F32), *(MFS[i, rows, cols] for i in range(3)))
            dst[n_unit] = new_master.astype(BF16)

    near_first = (1, 7, 2, 6, 3, 5, 4)

    class Stream:
        def __init__(self, name, bufs):
            self.axis, self.other, self.units = STREAMS[name]
            self.P, self.RL, self.RS, self.S2, self.R2, self.S3, self.R3, self.W = bufs
            self.two, self.near, self.long = {}, {}, {}
            self.ring_last = [arrival() for _ in range(Q)]
            self.gather_last = [arrival() for _ in range(Q)]
            self.back = [arrival() for _ in range(Q)]
            self.three = arrival()
            self.done = set()

        def half(self, r, q, h):
            return self.P[q].at[r, pl.ds(2 * h, 2)]

        def part(self, r, q, h):
            return self.W[q].at[r, pl.ds(2 * h, 2)]

        def places(self, xr, yr, kk, i):
            return (xr, yr, kk, i) if self.axis == "x" else (yr, xr, kk, i)

        def hop0(self, q):
            devs = both_ways(self.axis)
            self.near[q] = Group(
                [(self.half(2, q, w), self.RL[q].at[w], devs[w]) for w in range(2)], self.RL[q])
            Group(
                [(self.half(1 + 2 * w, q, 1 - w), self.RS[q].at[2 + w], devs[w]) for w in range(2)],
                self.RL[q], self.ring_last[q])

        def hop1(self, q):
            devs = both_ways(self.axis)
            self.near[q].arrive()
            for w in range(2):
                chunk = self.half(1 + 2 * w, q, w)
                add_rows(chunk, [chunk, self.RL[q].at[w]], 2)
            Group(
                [(self.half(1 + 2 * w, q, w), self.RS[q].at[w], devs[w]) for w in range(2)],
                self.RL[q], self.ring_last[q])

        def second(self, q):
            wait_bytes(self.RS[q], self.ring_last[q])
            for h in range(2):
                add_rows(
                    self.S2[q].at[pl.ds(2 * h, 2)], [self.half(0, q, h), self.RS[q].at[h], self.RS[q].at[3 - h]], 2)
            self.two[q] = spread(
                self.other, lambda r: self.S2[q].at[r], lambda r: self.R2[q].at[r - 1], (2, 1, 3), self.R2[q])

        def third(self, q):
            self.two[q].arrive()
            add_rows(self.S3.at[pl.ds(START[q], GROUPS[q])], [self.S2[q].at[0]] + [self.R2[q].at[r] for r in range(3)], GROUPS[q])
            order = [r for r in ORDER[START[q]:START[q] + GROUPS[q]] if r > 0]
            spread("z", lambda r: self.S3.at[PLACE[r]], lambda r: self.R3.at[r - 1], order,
                   self.S3.at[pl.ds(START[q], len(order))], self.three)

        def own(self, r):
            return self.W[GROUP[PLACE[r]]].at[0, 0, PLACE[r] - START[GROUP[PLACE[r]]]]

        def update(self):
            wait_bytes(self.R3, self.three)
            own_update(self.units, self.S3.at[7], self.R3, 7, self.own(0))
            spread("z", lambda r: self.own(0), lambda r: self.own(NZ - r), near_first, self.R3,
                   [self.back[GROUP[PLACE[NZ - r]]] for r in near_first])

        def across(self, q):
            came = len([r for r in ORDER[START[q]:START[q] + GROUPS[q]] if r > 0])
            wait_bytes(self.W[q].at[0, 0, pl.ds(0, came)], self.back[q])
            spread(
                self.other, lambda r: self.W[q].at[0, 0], lambda r: self.W[q].at[0, 4 - r], (2, 1, 3),
                self.W[q].at[0, pl.ds(1, 3)], self.near[q].recv)

        def go0(self, q):
            devs = both_ways(self.axis)
            wait_bytes(self.W[q].at[0, pl.ds(1, 3)], self.near[q].recv)
            self.long[q] = Group(
                [(self.part(0, q, w), self.part(3 - 2 * w, q, w), devs[w]) for w in range(2)], self.W[q].at[0])
            Group(
                [(self.part(0, q, 1 - w), self.part(3 - 2 * w, q, 1 - w), devs[w]) for w in range(2)],
                self.W[q].at[0], self.gather_last[q])

        def go1(self, q):
            devs = both_ways(self.axis)
            self.long[q].arrive()
            Group(
                [(self.part(3 - 2 * w, q, w), self.part(2, q, w), devs[w]) for w in range(2)],
                self.W[q].at[0], self.gather_last[q])

        def finish(self, q):
            if q not in self.done:
                self.done.add(q)
                wait_bytes(self.W[q].at[pl.ds(0, 2)], self.gather_last[q])

    streams = {name: Stream(name, bufs) for name, bufs in zip(STREAMS, (buf_x, buf_y))}
    x_s, y_s = streams.values()
    zs = {}

    def z_second():
        ring_z.long[3].arrive()
        ring_z.short[2].arrive()
        ring_z.total(lambda half: S2Z.at[pl.ds(2 * half, 2)])
        zs["two"] = spread("x", lambda r: S2Z.at[r], lambda r: R2Z.at[r - 1], (2, 1, 3), R2Z)

    def z_third():
        zs["two"].arrive()
        add_rows(S3Z, [S2Z.at[0], R2Z.at[0], R2Z.at[1], R2Z.at[2]], 4)
        zs["three"] = spread("y", lambda r: S3Z.at[r], lambda r: R3Z.at[r - 1], (2, 1, 3), R3Z)

    def z_update():
        zs["three"].arrive()
        own_update(Z_UNITS, S3Z.at[0], R3Z, 3, WZ.at[7, 0, 0])
        zs["back_y"] = spread(
            "y", lambda r: WZ.at[7, 0, 0], lambda r: WZ.at[7, 0, NY - r], (2, 1, 3), WZ.at[7, 0, pl.ds(1, 3)])

    def z_across():
        zs["back_y"].arrive()
        zs["back_x"] = spread(
            "x", lambda r: WZ.at[7, 0], lambda r: WZ.at[7, NX - r], (2, 1, 3), WZ.at[7, pl.ds(1, 3)])

    def z_gather(step):
        if step == 0:
            zs["back_x"].arrive()
        else:
            zs["gather", step - 1].arrive()
        devs = both_ways("z")
        items = []
        for way in range(2):
            r = (NZ - step) % NZ if way == 0 else step
            land = NZ - step - 1 if way == 0 else step + 1
            for half in ((0, 1) if step < 3 else (way,)):
                rows = pl.ds(2 * half, 2)
                items.append((WZ.at[PLACE[r], rows], WZ.at[PLACE[land], rows], devs[way]))
        zs["gather", step] = Group(items, WZ.at[pl.ds(0, 2)] if step < 3 else WZ.at[0])

    def states():
        wait_bytes(MFS, bulk_sem.at[3])

    def rows_1():
        zs["g1"] = spread(
            "x", lambda r: GB.at[0, 0, 0], lambda r: GB.at[0, 0, NX - r], (2, 1, 3), GB.at[0, 0, pl.ds(1, 3)])

    def rows_2():
        zs["g1"].arrive()
        zs["g2"] = Group([(GB.at[0, 0], GB.at[0, 1], ahead["y", 2])], GB.at[0, 0])

    def rows_3():
        zs["g2"].arrive()
        zs["g3"] = Group([(GB.at[0], GB.at[1], mate)], GB.at[0])

    def moments(cr):
        def body(i, carry):
            yr, xr = i // 4, lax.rem(i, 4)
            side = core if cr == 0 else 1 - core
            row = side * 256 + lax.rem(x + xr, NX) * 64 + lax.rem(y_hi + yr, 2) * 32
            rows = pl.ds(pl.multiple_of(row, 32), 32)
            new_master, new_first, new_second = adam(
                GB[cr, yr, xr].astype(F32), *(MFS[j, rows, :] for j in range(3)))
            o_master[rows, :] = new_master
            o_first[rows, :] = new_first
            o_second[rows, :] = new_second
            return carry
        lax.fori_loop(0, 8, body, 0)

    v_sem = arrival()

    def values(part):
        blocks, first = GROUPS[part], START[part]
        for st in streams.values():
            st.finish(part)
        for step in range(max(min(r, NZ - r) for r in ORDER[first:first + blocks])):
            zs["gather", step].arrive()

        def body(j, carry):
            y_lo = lax.rem(j, 2)
            k = first + j // 2
            for g, xr, yr in groups(y_lo):
                def put(unit, w):
                    row, col = unit
                    at = pl.ds(pl.multiple_of(j * 256 + g * 32 + row * 16, 16), 16)
                    WT[at, col * 128:col * 128 + 128] = w
                for st in streams.values():
                    for i, unit in enumerate(st.units):
                        put(unit, st.W[part][st.places(xr, yr, j // 2, i)])
                for i, unit in enumerate(Z_UNITS):
                    put(unit, WZ[k, xr, yr, i])
            return carry
        lax.fori_loop(0, 2 * blocks, body, 0)
        cols, rows = pl.ds(first * 512, blocks * 512), pl.ds(0, blocks * 512)
        if part == Q - 1:
            VO[...] = jnp.dot(NB[:, cols], WT[rows, :], preferred_element_type=F32)
        elif part > 0:
            VO[...] += jnp.dot(NB[:, cols], WT[rows, :], preferred_element_type=F32)
        else:
            theirs, ours = pl.ds(128, 128), pl.ds(0, 128)
            VO[theirs, :] += jnp.dot(NB[theirs, cols], WT[rows, :], preferred_element_type=F32)
            Group([(VO.at[theirs], VR, mate)], VR, v_sem)
            VO[ours, :] += jnp.dot(NB[ours, cols], WT[rows, :], preferred_element_type=F32)

    def nexts():
        wait_bytes(NB, bulk_sem.at[2])

    def last_swap():
        wait_bytes(VR, v_sem)
        o_values[...] = (VO[pl.ds(0, 128), :] + VR[...]).astype(BF16)

    wait_bytes(CB, c_sem)
    gemm(0, 1)
    z_long(0)
    y_s.hop0(0)
    x_s.hop0(0)
    gemm(1, 3)
    x_s.hop0(1)
    y_s.hop0(1)
    z_short(0)
    gemm(3, 5)
    y_s.hop1(0)
    y_s.hop0(2)
    x_s.hop1(0)
    x_s.hop0(2)
    z_long(1)
    gemm(5, 8)
    x_s.hop1(1)
    states()
    z_short(1)
    y_s.hop1(1)
    x_s.hop0(3)
    y_s.second(0)
    y_s.hop0(3)
    x_s.second(0)
    x_s.hop1(2)
    z_long(2)
    y_s.hop1(2)
    z_short(2)
    x_s.hop1(3)
    z_long(3)
    x_s.second(1)
    y_s.second(1)
    y_s.hop1(3)
    y_s.second(2)
    y_s.third(0)
    x_s.third(0)
    x_s.second(2)
    z_second()
    x_s.second(3)
    y_s.second(3)
    x_s.third(1)
    x_s.third(2)
    y_s.third(1)
    z_third()
    x_s.third(3)
    y_s.third(2)
    y_s.third(3)
    x_s.update()
    z_update()
    nexts()
    y_s.update()
    rows_1()
    x_s.across(3)
    z_across()
    x_s.across(2)
    y_s.across(3)
    rows_2()
    y_s.across(2)
    x_s.across(1)
    z_gather(0)
    y_s.across(1)
    x_s.go0(3)
    x_s.across(0)
    y_s.go0(3)
    y_s.across(0)
    y_s.go0(2)
    x_s.go0(1)
    z_gather(1)
    y_s.go0(1)
    rows_3()
    moments(0)
    x_s.go0(2)
    y_s.go1(3)
    zs["g3"].arrive()
    moments(1)
    y_s.go0(0)
    x_s.go0(0)
    y_s.go1(2)
    x_s.go1(3)
    z_gather(2)
    x_s.go1(2)
    y_s.go1(1)
    x_s.go1(1)
    z_gather(3)
    x_s.go1(0)
    y_s.go1(0)
    values(3)
    values(2)
    values(1)
    values(0)
    last_swap()
    for group in pool:
        if group is not None:
            group.leave()
    wait_bytes(XB.at[pl.ds(0, 8)], bulk_sem.at[0])
    wait_bytes(NB.at[pl.ds(0, 128)], bulk_sem.at[1])


def place(a, b, c, d, o_a, o_b, o_c, o_d, sem):
    copies = [
        pltpu.make_async_copy(src, dst, sem.at[i])
        for i, (src, dst) in enumerate(((a, o_a), (b, o_b), (c, o_c), (d, o_d)))
    ]
    for copy in copies:
        copy.start()
    for copy in copies:
        copy.wait()


OUTS = (((512, 512), F32), ((512, 512), F32), ((512, 512), F32), ((128, 512), BF16))


def local_step(layer_input, value_cotangent, master_weight, first_moment, second_moment, next_input):
    unit = (16, 128)

    def vm(*shape, dtype=BF16):
        return pltpu.VMEM(shape, dtype)

    def stream_buffers(n):
        u = (n,) + unit
        def each(*dims):
            return tuple(vm(*dims, size, *u) for size in GROUPS)

        return (each(4, 4), each(2, 2), each(4, 2), each(4), each(3), vm(8, *u), vm(7, *u), each(4, 4))

    half_z = (2, 4, 2) + unit
    scratch = [
        vm(16, 1024, 256), vm(1024, 512), vm(256, 4096),
        vm(8, 4, 4, 2, *unit), vm(4, 2, *half_z), vm(3, 2, *half_z),
        vm(4, 4, 2, *unit), vm(3, 4, 2, *unit), vm(4, 2, *unit), vm(3, 2, *unit), vm(8, 4, 4, 2, *unit),
        *[stream_buffers(len(STREAMS[name][2])) for name in STREAMS],
        vm(2, 2, 4, 32, 512),
        vm(3, 512, 512, dtype=F32),
        vm(512 * max(GROUPS), 512), vm(256, 512, dtype=F32), vm(128, 512, dtype=F32),
        pltpu.SemaphoreType.DMA((POOL,)), pltpu.SemaphoreType.DMA((ARRIVALS,)),
        pltpu.SemaphoreType.DMA((16,)), pltpu.SemaphoreType.DMA((4,)),
    ]
    results = pl.pallas_call(
        kernel,
        out_shape=tuple(pltpu.VMEM(shape, dtype) for shape, dtype in OUTS),
        in_specs=[pl.BlockSpec(memory_space=pl.ANY)] * 6,
        out_specs=(pl.BlockSpec(memory_space=pltpu.VMEM),) * 4,
        scratch_shapes=scratch,
        compiler_params=pltpu.CompilerParams(
            collective_id=0, has_side_effects=True, vmem_limit_bytes=56 * 2**20),
        cost_estimate=pl.CostEstimate(flops=5_400_000_000, bytes_accessed=18_000_000, transcendentals=0),
        name="value_projection_step",
    )(layer_input, value_cotangent, master_weight, first_moment, second_moment, next_input)
    return tuple(pl.pallas_call(
        place,
        out_shape=tuple(jax.ShapeDtypeStruct(shape, dtype) for shape, dtype in OUTS),
        in_specs=[pl.BlockSpec(memory_space=pltpu.VMEM)] * 4,
        out_specs=(pl.BlockSpec(memory_space=pl.ANY),) * 4,
        scratch_shapes=[pltpu.SemaphoreType.DMA((4,))],
        compiler_params=pltpu.CompilerParams(vmem_limit_bytes=2**20),
        name="place_results",
    )(*results))


def solution(mesh):
    in_specs = (
        P(("cuts", "fsdp"), None),
        P(("cuts", "fsdp"), None),
        P("fsdp", None),
        P("fsdp", None),
        P("fsdp", None),
        P(("cuts", "fsdp"), None),
    )
    out_specs = (P("fsdp", None), P("fsdp", None), P("fsdp", None), P(("cuts", "fsdp"), None))
    return jax.shard_map(local_step, mesh=mesh, in_specs=in_specs, out_specs=out_specs, check_vma=False)
```
